32 devices in a mesh: grp: 8 (over z, core), blk: 4 (over y, x).
Axes of the slice: x: 2, y: 2, z: 4, core: 2. Of those that a mesh axis runs over, the one named last changes fastest.
Arguments:
- child_inverse: bfloat16 [8, 2, 2048, 2048], P('grp', None, 'blk'), may hold values from -0.09375 to 0.09375
- border_block: bfloat16 [8, 2, 2048, 2048], P('grp', None, 'blk'), may hold values from -0.09375 to 0.09375
- child_rhs: bfloat16 [8, 2, 2048, 256], P('grp', None, 'blk'), may hold values from -6 to 6
- parent_inverse: bfloat16 [8, 2, 4096, 2048], P('grp', None, 'blk'), may hold values from -0.0625 to 0.0625
- parent_rhs: bfloat16 [8, 2, 2048, 256], P('grp', None, 'blk'), may hold values from -6 to 6
- parent_of: int32 [8, 1], replicated, may hold values from 0 to 3
- owner: int32 [4], replicated, may hold values from 0 to 3, each once
- row_map: int32 [8, 2048], replicated, may hold values from 0 to 4095, as said below
Outputs:
- child_solution: bfloat16 [8, 2, 2048, 256], P('grp', None, 'blk')
- parent_solution: bfloat16 [8, 2, 2048, 256], P('grp', None, 'blk')
The draws below stay inside these ranges and needn't reach their ends.
Inputs may be any that keep to these rules, and one draw needn't show every extreme that they name: parent_of[c, 0] is the parent front of the sibling front on group c; every parent front has one sibling or more. owner[p] names the pair of groups 2 owner[p] and 2 owner[p] + 1 that holds parent front p; each pair holds one parent. row_map[c, j] differ for different j of one c; border row j with j // 512 = b goes to a parent row h * 2048 + b * 512 + r with h of 0 or 1 and r < 512.
All inputs are finite; a program needn't handle non-finite values.
Results may differ from the reference program's by a relative error of at most 0.008.
Values may be sent and summed in bfloat16 or wider, within the bound.
A program may use at most 64 MiB of HBM per device.

```python
import jax
import jax.numpy as jnp
from jax import lax

PIV = 2048
BORDER = 2048
PPIV = 4096
SRC = 256
GROUPS = 8
PARENTS = 4
BROWS = 512
PROWS = 512


def draw_row_map(key, part):
    slices_count = BORDER // BROWS
    slot_total = GROUPS * slices_count
    slot_keys = jax.random.split(jax.random.fold_in(key, 7), slot_total)
    orders = jax.vmap(lambda single_key: jax.random.permutation(single_key, 2 * PROWS))(slot_keys)
    slot_ids = jnp.arange(slot_total)
    target_ids = jnp.where(slot_ids == 0, 0, jnp.where(slot_ids == slices_count - 1, 2 * PROWS - 1, -1))
    leading = orders[:, :1]
    orders = jnp.where(orders == target_ids[:, None], leading, orders)
    orders = orders.at[:, 0].set(jnp.where(target_ids >= 0, target_ids, orders[:, 0]))
    chosen = orders[:, :BROWS]
    half_index = chosen // PROWS
    offsets = chosen % PROWS
    block_index = (slot_ids % slices_count)[:, None]
    parent_row = half_index * (PPIV // 2) + block_index * PROWS + offsets
    return parent_row.reshape(GROUPS, BORDER).astype(jnp.int32)


def block_scale(key, extent, cuts, least, high):
    def one(dim, blocks):
        steps = jax.random.uniform(jax.random.fold_in(jax.random.fold_in(key, 6), dim), (blocks,), jnp.float32, least / len(cuts), high / len(cuts))
        return jnp.repeat(jnp.exp(steps), extent[dim] // blocks).reshape((-1,) + (1,) * (len(extent) - dim - 1))

    factor_of = one(*cuts[0])
    for cut in cuts[1:]:
        factor_of = factor_of * one(*cut)
    return factor_of


def picks_of(rng, rows, number_of, top, lift):
    ranking = jax.random.permutation(jax.random.fold_in(rng, 1), number_of)
    pull = ranking
    for power in range(3):
        pull = pull * pull // number_of
    pull = pull * lift // number_of
    tickets = jax.random.randint(jax.random.fold_in(rng, 2), (rows, number_of), 0, 4096) + pull
    fixed_rows = jax.random.permutation(jax.random.fold_in(rng, 3), rows)[jnp.arange(number_of) % rows]
    tickets = jnp.where(jnp.arange(rows)[:, None] == fixed_rows[None, :], 1 << 14, tickets)
    merit = tickets * number_of + jnp.arange(number_of)
    return lax.top_k(merit.astype(jnp.int32), top)[1].astype(jnp.int32)


def normal_values(key, shape, width, bound, pieces=(), kind=jnp.bfloat16):
    values = width * jax.random.normal(key, shape, jnp.float32)
    if pieces:
        values = values * block_scale(key, shape, pieces, -0.22, 0.18)
    return jnp.clip(values, -bound, bound).astype(kind)


def setup_inputs(seed: int = 0) -> dict:
    key_of = jax.random.split(jax.random.key(seed), 9)
    child_inverse = normal_values(key_of[0], (GROUPS, 2, PIV, PIV), (2 * PIV) ** -0.5, 0.09375, ((0, 8), (2, 4)))
    border_block = normal_values(key_of[1], (GROUPS, 2, BORDER, PIV), (2 * PIV) ** -0.5, 0.09375, ((0, 8), (2, 4)))
    child_rhs = normal_values(key_of[2], (GROUPS, 2, PIV, SRC), 1.0, 6.0, ((0, 8), (2, 4)))
    parent_inverse = normal_values(key_of[3], (GROUPS, 2, PPIV, PPIV // 2), (2 * PPIV) ** -0.5, 0.0625, ((0, 8), (2, 4)))
    parent_rhs = normal_values(key_of[4], (GROUPS, 2, PPIV // 2, SRC), 1.0, 6.0, ((0, 8), (2, 4)))
    parent_of = picks_of(key_of[5], GROUPS, PARENTS, 1, 4096)
    owner = jax.random.permutation(key_of[6], PARENTS).astype(jnp.int32)
    row_map = draw_row_map(jax.random.fold_in(key_of[8], 71), 0)
    return {"child_inverse": child_inverse, "border_block": border_block, "child_rhs": child_rhs, "parent_inverse": parent_inverse, "parent_rhs": parent_rhs, "parent_of": parent_of, "owner": owner, "row_map": row_map}


def complex_product(left, right):
    real_part = jnp.dot(left[0], right[0], preferred_element_type=jnp.float32) - jnp.dot(left[1], right[1], preferred_element_type=jnp.float32)
    imag_part = jnp.dot(left[0], right[1], preferred_element_type=jnp.float32) + jnp.dot(left[1], right[0], preferred_element_type=jnp.float32)
    return jnp.stack([real_part, imag_part])


def reference(child_inverse, border_block, child_rhs, parent_inverse, parent_rhs, parent_of, owner, row_map):
    def solve_child(element):
        inverse_part, border_part, source_part = element
        solved = complex_product(inverse_part, source_part).astype(jnp.bfloat16)
        update_part = (-complex_product(border_part, solved)).astype(jnp.bfloat16)
        return solved, update_part

    child_solution, updates = lax.map(solve_child, (child_inverse, border_block, child_rhs))
    pair_of_child = owner[parent_of[:, 0]].astype(jnp.int32)

    def add_child(totals, element):
        update_part, pair_index, row_list = element
        front_rows = totals[pair_index]
        front_rows = front_rows.at[:, row_list, :].add(update_part.astype(jnp.float32))
        return totals.at[pair_index].set(front_rows), None

    zero_sums = jnp.zeros((PARENTS, 2, PPIV, SRC), jnp.float32)
    sums, unused = lax.scan(add_child, zero_sums, (updates, pair_of_child, row_map.astype(jnp.int32)))
    own_rhs = parent_rhs.reshape(PARENTS, 2, 2, PPIV // 2, SRC).transpose(0, 2, 1, 3, 4).reshape(PARENTS, 2, PPIV, SRC)
    right_side = (own_rhs.astype(jnp.float32) + sums).astype(jnp.bfloat16)
    inverse_halves = parent_inverse.reshape(PARENTS, 2, 2, PPIV, PPIV // 2)

    def solve_parent(element):
        halves, rhs_part = element
        full_inverse = jnp.concatenate([halves[0], halves[1]], axis=-1)
        return complex_product(full_inverse, rhs_part)

    solved_parent = lax.map(solve_parent, (inverse_halves, right_side))
    blocks_count = PPIV // (2 * PROWS)
    arranged = solved_parent.reshape(PARENTS, 2, blocks_count, 2, PROWS, SRC).transpose(0, 3, 1, 2, 4, 5)
    parent_solution = arranged.reshape(GROUPS, 2, PPIV // 2, SRC).astype(jnp.bfloat16)
    return child_solution, parent_solution
```

```python
import functools

import jax
import jax.numpy as jnp
from jax import lax
from jax.experimental import pallas as pl
from jax.experimental.pallas import tpu as pltpu
from jax.sharding import PartitionSpec as P

MESH = pl.DeviceIdType.MESH
LANES = 128


def tile_of(rows):
    return 256 if rows % 256 == 0 else rows


def complex_rows(matrix, first, tile, block):
    depth = matrix.shape[2]
    half = block.shape[1] // 2
    left = matrix[:, pl.ds(first, tile), :].reshape(2 * tile, depth)
    both = jnp.dot(left, block[...], preferred_element_type=jnp.float32)
    real_part = both[:tile, :half] - both[tile:, half:]
    imag_part = both[:tile, half:] + both[tile:, :half]
    return jnp.concatenate([real_part, imag_part], axis=1)


def kernel(
    slots,
    groups,
    inverse_hbm,
    border_hbm,
    rhs_hbm,
    parent_hbm,
    parent_rhs_hbm,
    parent_of,
    owner,
    row_map_hbm,
    child_out,
    parent_out,
    inverse,
    border,
    parent,
    parent_rhs,
    row_map,
    gather_rhs,
    gather_sol,
    gather_right,
    updates,
    onehot,
    half_out,
    half_in,
    last_out,
    last_in,
    result,
    ag_send,
    ag_recv,
    z_send,
    z_recv,
    h_send,
    h_recv,
    y_send,
    y_recv,
    load_sem,
    own_sem,
    store_sem,
):
    pairs = groups // 2
    g = lax.axis_index("grp")
    b = lax.axis_index("blk")
    core = lax.rem(g, 2)
    k = lax.div(g, 2)
    chunks = gather_rhs.shape[0]
    bits = slots.bit_length() - 1
    child_rows = inverse.shape[1]
    border_rows = border.shape[1]
    half_rows = parent_rhs.shape[1]
    half_order = parent.shape[2]
    out_rows = result.shape[1]

    def flipped(mask):
        index = b
        for bit in range(bits):
            if mask >> bit & 1:
                index = index + (1 << bit) * (1 - 2 * lax.rem(lax.div(index, 1 << bit), 2))
        return index

    partner = g + 1 - 2 * core

    loads = [
        pltpu.make_async_copy(src, dst, load_sem.at[i])
        for i, (src, dst) in enumerate(
            [
                (row_map_hbm.at[:, pl.ds(pl.multiple_of(b * border_rows, LANES), border_rows)], row_map),
                (inverse_hbm.at[0], inverse),
                (border_hbm.at[0], border),
                (parent_rhs_hbm.at[0], parent_rhs),
                (parent_hbm.at[0], parent),
            ]
        )
    ]
    own_copies = []
    for ch in range(chunks):
        for p in range(2):
            own_copies.append(
                pltpu.make_async_copy(
                    rhs_hbm.at[0, p, :, pl.ds(ch * LANES, LANES)],
                    gather_rhs.at[
                        ch,
                        pl.ds(pl.multiple_of(b * child_rows, child_rows), child_rows),
                        pl.ds(p * LANES, LANES),
                    ],
                    own_sem.at[ch * 2 + p],
                )
            )
    for copy in own_copies:
        copy.start()
    for copy in loads:
        copy.start()

    barrier = pltpu.get_barrier_semaphore()
    for bit in range(bits):
        pl.semaphore_signal(barrier, inc=1, device_id=(g, flipped(1 << bit)), device_id_type=MESH)
    for d in range(1, pairs):
        peer = lax.rem(k + d, pairs) * 2 + core
        pl.semaphore_signal(barrier, inc=1, device_id=(peer, b), device_id_type=MESH)
    pl.semaphore_signal(barrier, inc=1, device_id=(partner, b), device_id_type=MESH)
    pl.semaphore_wait(barrier, bits + pairs)

    orders = (tuple(range(bits)), tuple(reversed(range(bits))))
    buffers = (gather_rhs, gather_sol, gather_right)

    def via(p, mask):
        return [bit for bit in orders[p] if mask >> bit & 1][-1]

    def shard(stage, ch, p, index):
        rows = buffers[stage].shape[1] // slots
        return buffers[stage].at[
            ch, pl.ds(pl.multiple_of(index * rows, rows), rows), pl.ds(p * LANES, LANES)
        ]

    def hop(stage, ch, p, mask):
        bit = via(p, mask)
        held = mask & ~(1 << bit)
        origin = flipped(held)
        place = shard(stage, ch, p, origin)
        source = place
        if stage == 0 and held == 0:
            source = rhs_hbm.at[0, p, :, pl.ds(ch * LANES, LANES)]
        return pltpu.make_async_remote_copy(
            src_ref=source,
            dst_ref=place,
            send_sem=ag_send.at[stage, ch, p, mask],
            recv_sem=ag_recv.at[stage, ch, p, mask],
            device_id=(g, flipped(1 << bit)),
            device_id_type=MESH,
        )

    def gather_start(stage, ch):
        for first in (True, False):
            for p in range(2):
                for bit in orders[p]:
                    if (bit == orders[p][0]) == first:
                        hop(stage, ch, p, 1 << bit).start()

    def gather_forward(stage, ch):
        for step in range(1, bits):
            for p in range(2):
                early = [bit for bit in orders[p][:step]]
                for mask in range(1, slots):
                    if mask >> orders[p][step - 1] & 1 and not any(
                        mask >> bit & 1 for bit in orders[p][step:]
                    ):
                        assert early
                        hop(stage, ch, p, mask).wait_recv()
                        for bit in orders[p][step:]:
                            hop(stage, ch, p, mask | 1 << bit).start()

    def gather_finish(stage, ch):
        for p in range(2):
            for mask in range(1, slots):
                if mask >> orders[p][-1] & 1:
                    hop(stage, ch, p, mask).wait_recv()

    def gather_drain(stage, ch):
        for p in range(2):
            for mask in range(1, slots):
                hop(stage, ch, p, mask).wait_send()

    def update_slot(ch, index):
        return updates.at[ch, pl.ds(pl.multiple_of(index * border_rows, border_rows), border_rows), :]

    def update_copy(ch, d):
        return pltpu.make_async_remote_copy(
            src_ref=update_slot(ch, k),
            dst_ref=update_slot(ch, k),
            send_sem=z_send.at[ch, d],
            recv_sem=z_recv.at[ch, d],
            device_id=(lax.rem(k + d, pairs) * 2 + core, b),
            device_id_type=MESH,
        )

    def swap_copy(source, target, send_sem, recv_sem, ch):
        return pltpu.make_async_remote_copy(
            src_ref=source.at[ch],
            dst_ref=target.at[ch],
            send_sem=send_sem.at[ch],
            recv_sem=recv_sem.at[ch],
            device_id=(partner, b),
            device_id_type=MESH,
        )

    def half_copy(ch):
        return swap_copy(half_out, half_in, h_send, h_recv, ch)

    def last_copy(ch):
        return swap_copy(last_out, last_in, y_send, y_recv, ch)

    def solve_child(ch):
        tile = tile_of(child_rows)

        @pl.loop(0, child_rows // tile)
        def _(i):
            value = complex_rows(inverse, pl.multiple_of(i * tile, tile), tile, gather_rhs.at[ch])
            row = pl.multiple_of(b * child_rows + i * tile, tile)
            gather_sol[ch, pl.ds(row, tile), :] = value.astype(jnp.bfloat16)

    def make_updates(ch):
        tile = tile_of(border_rows)

        @pl.loop(0, border_rows // tile)
        def _(i):
            value = complex_rows(border, pl.multiple_of(i * tile, tile), tile, gather_sol.at[ch])
            row = pl.multiple_of(k * border_rows + i * tile, tile)
            updates[ch, pl.ds(row, tile), :] = (-value).astype(jnp.bfloat16)

    def add_updates(ch):
        tile = tile_of(half_rows)

        @pl.loop(0, half_rows // tile)
        def _(i):
            row = pl.multiple_of((1 - core) * half_rows + i * tile, tile)
            value = jnp.dot(
                onehot[pl.ds(row, tile), :], updates[ch], preferred_element_type=jnp.float32
            )
            half_out[ch, pl.ds(pl.multiple_of(i * tile, tile), tile), :] = value.astype(jnp.bfloat16)

        half_copy(ch).start()
        half_copy(ch).wait_recv()

        @pl.loop(0, half_rows // tile)
        def _(i):
            here = pl.ds(pl.multiple_of(i * tile, tile), tile)
            row = pl.multiple_of(core * half_rows + i * tile, tile)
            value = jnp.dot(
                onehot[pl.ds(row, tile), :], updates[ch], preferred_element_type=jnp.float32
            )
            value = value + half_in[ch, here, :].astype(jnp.float32)
            own = parent_rhs[:, here, pl.ds(ch * LANES, LANES)].astype(jnp.float32)
            value = value + jnp.concatenate([own[0], own[1]], axis=1)
            place = pl.multiple_of(b * half_rows + i * tile, tile)
            gather_right[ch, pl.ds(place, tile), :] = value.astype(jnp.bfloat16)

    def solve_parent(ch):
        tile = tile_of(out_rows)

        @pl.loop(0, out_rows // tile)
        def _(i):
            first = pl.multiple_of((1 - core) * out_rows + i * tile, tile)
            value = complex_rows(parent, first, tile, gather_right.at[ch])
            last_out[ch, pl.ds(pl.multiple_of(i * tile, tile), tile), :] = value.astype(jnp.bfloat16)

        last_copy(ch).start()
        last_copy(ch).wait_recv()

        @pl.loop(0, out_rows // tile)
        def _(i):
            here = pl.ds(pl.multiple_of(i * tile, tile), tile)
            first = pl.multiple_of(core * out_rows + i * tile, tile)
            value = complex_rows(parent, first, tile, gather_right.at[ch])
            value = (value + last_in[ch, here, :].astype(jnp.float32)).astype(jnp.bfloat16)
            result[0, here, pl.ds(ch * LANES, LANES)] = value[:, :LANES]
            result[1, here, pl.ds(ch * LANES, LANES)] = value[:, LANES:]

    def child_store(ch, p):
        return pltpu.make_async_copy(
            shard(1, ch, p, b),
            child_out.at[0, p, :, pl.ds(ch * LANES, LANES)],
            store_sem.at[ch * 2 + p],
        )

    def parent_store(ch):
        lanes = pl.ds(ch * LANES, LANES)
        return pltpu.make_async_copy(
            result.at[:, :, lanes], parent_out.at[0, :, :, lanes], store_sem.at[2 * chunks + ch]
        )

    gather_start(0, 0)
    loads[0].wait()
    tile = tile_of(half_rows)
    for other in range(pairs):
        group = 2 * other + core
        mine = owner[parent_of[group, 0]] == k
        wanted = jnp.where(mine, row_map[pl.ds(group, 1), :], -1)

        @pl.loop(0, 2 * half_rows // tile)
        def _(i):
            first = i * tile
            base = lax.div(first, half_rows) * half_order + b * half_rows + lax.rem(first, half_rows)
            rows = base + lax.broadcasted_iota(jnp.int32, (tile, border_rows), 0)
            hits = jnp.where(rows == wanted, 1.0, 0.0).astype(jnp.bfloat16)
            onehot[
                pl.ds(pl.multiple_of(first, tile), tile),
                other * border_rows : (other + 1) * border_rows,
            ] = hits

    gather_forward(0, 0)
    for ch in range(1, chunks):
        gather_start(0, ch)
    loads[1].wait()
    for ch in range(chunks):
        if ch:
            gather_forward(0, ch)
        gather_finish(0, ch)
        own_copies[2 * ch].wait()
        own_copies[2 * ch + 1].wait()
        solve_child(ch)
        gather_start(1, ch)
        child_store(ch, 0).start()
        child_store(ch, 1).start()
    loads[2].wait()
    for ch in range(chunks):
        gather_forward(1, ch)
        gather_finish(1, ch)
        make_updates(ch)
        for d in range(1, pairs):
            update_copy(ch, d).start()
    loads[3].wait()
    for ch in range(chunks):
        for d in range(1, pairs):
            update_copy(ch, d).wait_recv()
        add_updates(ch)
        gather_start(2, ch)
    loads[4].wait()
    for ch in range(chunks):
        gather_forward(2, ch)
        gather_finish(2, ch)
        solve_parent(ch)
        parent_store(ch).start()
    for ch in range(chunks):
        for stage in range(3):
            gather_drain(stage, ch)
        for d in range(1, pairs):
            update_copy(ch, d).wait_send()
        half_copy(ch).wait_send()
        last_copy(ch).wait_send()
        child_store(ch, 0).wait()
        child_store(ch, 1).wait()
        parent_store(ch).wait()


def per_device(
    slots,
    groups,
    child_inverse,
    border_block,
    child_rhs,
    parent_inverse,
    parent_rhs,
    parent_of,
    owner,
    row_map,
):
    sources = child_rhs.shape[3]
    chunks = sources // LANES
    pairs = groups // 2
    child_rows = child_inverse.shape[2]
    border_rows = border_block.shape[2]
    half_rows = parent_rhs.shape[2]
    out_rows = parent_inverse.shape[2] // 2
    both = 2 * LANES
    bf16 = jnp.bfloat16
    dma = pltpu.SemaphoreType.DMA
    anywhere = pl.BlockSpec(memory_space=pl.ANY)
    scalars = pl.BlockSpec(memory_space=pltpu.SMEM)
    return pl.pallas_call(
        functools.partial(kernel, slots, groups),
        out_shape=(
            jax.ShapeDtypeStruct((1, 2, child_rows, sources), bf16),
            jax.ShapeDtypeStruct((1, 2, out_rows, sources), bf16),
        ),
        in_specs=[anywhere] * 5 + [scalars, scalars, anywhere],
        out_specs=(anywhere, anywhere),
        scratch_shapes=[
            pltpu.VMEM(child_inverse.shape[1:], bf16),
            pltpu.VMEM(border_block.shape[1:], bf16),
            pltpu.VMEM(parent_inverse.shape[1:], bf16),
            pltpu.VMEM(parent_rhs.shape[1:], bf16),
            pltpu.VMEM((groups, border_rows), jnp.int32),
            pltpu.VMEM((chunks, slots * child_rows, both), bf16),
            pltpu.VMEM((chunks, slots * child_rows, both), bf16),
            pltpu.VMEM((chunks, slots * half_rows, both), bf16),
            pltpu.VMEM((chunks, pairs * border_rows, both), bf16),
            pltpu.VMEM((2 * half_rows, pairs * border_rows), bf16),
            pltpu.VMEM((chunks, half_rows, both), bf16),
            pltpu.VMEM((chunks, half_rows, both), bf16),
            pltpu.VMEM((chunks, out_rows, both), bf16),
            pltpu.VMEM((chunks, out_rows, both), bf16),
            pltpu.VMEM((2, out_rows, sources), bf16),
            dma((3, chunks, 2, slots)),
            dma((3, chunks, 2, slots)),
            dma((chunks, pairs)),
            dma((chunks, pairs)),
            dma((chunks,)),
            dma((chunks,)),
            dma((chunks,)),
            dma((chunks,)),
            dma((5,)),
            dma((2 * chunks,)),
            dma((3 * chunks,)),
        ],
        compiler_params=pltpu.CompilerParams(
            collective_id=0, has_side_effects=True, vmem_limit_bytes=56 * 1024 * 1024
        ),
    )(child_inverse, border_block, child_rhs, parent_inverse, parent_rhs, parent_of, owner, row_map)


def solution(mesh):
    in_specs = (
        P("grp", None, "blk", None),
        P("grp", None, "blk", None),
        P("grp", None, "blk", None),
        P("grp", None, "blk", None),
        P("grp", None, "blk", None),
        P(),
        P(),
        P(),
    )
    out_specs = (P("grp", None, "blk", None), P("grp", None, "blk", None))
    return jax.shard_map(
        functools.partial(per_device, mesh.shape["blk"], mesh.shape["grp"]),
        mesh=mesh,
        in_specs=in_specs,
        out_specs=out_specs,
        check_vma=False,
    )
```

```python
import functools

import jax
import jax.numpy as jnp
from jax import lax
from jax.experimental import pallas as pl
from jax.experimental.pallas import tpu as pltpu
from jax.sharding import PartitionSpec as P

MESH = pl.DeviceIdType.MESH
LANES = 128


def tile_of(rows):
    return 256 if rows % 256 == 0 else rows


def kernel(
    slots,
    groups,
    inverse_hbm,
    border_hbm,
    rhs_hbm,
    parent_hbm,
    parent_rhs_hbm,
    parent_of,
    owner,
    row_map_hbm,
    child_out,
    parent_out,
    inverse,
    border,
    parent,
    parent_rhs,
    row_map,
    gather_rhs,
    gather_sol,
    gather_right,
    updates,
    onehot,
    total,
    parent_total,
    right_total,
    half_out,
    half_in,
    last_out,
    last_in,
    result,
    ag_send,
    ag_recv,
    right_send,
    right_recv,
    left_send,
    left_recv,
    h_send,
    h_recv,
    y_send,
    y_recv,
    load_sem,
    own_sem,
    store_sem,
):
    pairs = groups // 2
    g = lax.axis_index("grp")
    b = lax.axis_index("blk")
    core = lax.rem(g, 2)
    k = lax.div(g, 2)
    chunks = gather_rhs.shape[0]
    bits = slots.bit_length() - 1
    child_rows = inverse.shape[1]
    border_rows = border.shape[1]
    half_rows = parent_rhs.shape[1]
    half_order = parent.shape[2]
    out_rows = result.shape[1]
    bf16 = jnp.bfloat16
    f32 = jnp.float32

    def flipped(mask):
        index = b
        for bit in range(bits):
            if mask >> bit & 1:
                index = index + (1 << bit) * (1 - 2 * lax.rem(lax.div(index, 1 << bit), 2))
        return index

    partner = g + 1 - 2 * core
    has_left = k > 0
    has_right = k < pairs - 1

    loads = [
        pltpu.make_async_copy(src, dst, load_sem.at[i])
        for i, (src, dst) in enumerate(
            [
                (row_map_hbm.at[:, pl.ds(pl.multiple_of(b * border_rows, LANES), border_rows)], row_map),
                (inverse_hbm.at[0], inverse),
                (border_hbm.at[0], border),
                (parent_rhs_hbm.at[0], parent_rhs),
                (parent_hbm.at[0], parent),
            ]
        )
    ]
    own_copies = [
        pltpu.make_async_copy(
            rhs_hbm.at[0, p, :, pl.ds(ch * LANES, LANES)],
            gather_rhs.at[ch, p, pl.ds(pl.multiple_of(b * child_rows, child_rows), child_rows), :],
            own_sem.at[ch * 2 + p],
        )
        for ch in range(chunks)
        for p in range(2)
    ]

    barrier = pltpu.get_barrier_semaphore()
    for bit in range(bits):
        pl.semaphore_signal(barrier, inc=1, device_id=(g, flipped(1 << bit)), device_id_type=MESH)
    pl.semaphore_signal(barrier, inc=1, device_id=(partner, b), device_id_type=MESH)

    @pl.when(has_left)
    def _():
        pl.semaphore_signal(barrier, inc=1, device_id=(g - 2, b), device_id_type=MESH)

    @pl.when(has_right)
    def _():
        pl.semaphore_signal(barrier, inc=1, device_id=(g + 2, b), device_id_type=MESH)

    for copy in own_copies[:2] + loads[:2] + own_copies[2:] + loads[2:]:
        copy.start()
    neighbours = bits + 1 + jnp.where(has_left, 1, 0) + jnp.where(has_right, 1, 0)
    pl.semaphore_wait(barrier, neighbours)

    orders = (tuple(range(bits)), tuple(reversed(range(bits))))
    buffers = (gather_rhs, gather_sol, gather_right)
    arrived = set()
    sent = []
    by_size = sorted(range(slots), key=lambda mask: (mask.bit_count(), mask))

    def shard(stage, ch, p, index, half=None):
        rows = buffers[stage].shape[2] // slots
        count = rows if half is None else rows // 2
        first = pl.multiple_of(index * rows, rows)
        if half:
            first = pl.multiple_of(first + count, count)
        return buffers[stage].at[ch, p, pl.ds(first, count), :]

    def hop(stage, ch, p, half, mask):
        bit = [one for one in orders[half] if mask >> one & 1][-1]
        held = mask & ~(1 << bit)
        place = shard(stage, ch, p, flipped(held), half)
        source = place
        if stage == 0 and held == 0:
            count = child_rows // 2
            source = rhs_hbm.at[0, p, pl.ds(half * count, count), pl.ds(ch * LANES, LANES)]
        return pltpu.make_async_remote_copy(
            src_ref=source,
            dst_ref=place,
            send_sem=ag_send.at[stage, ch, p, half, mask],
            recv_sem=ag_recv.at[stage, ch, p, half, mask],
            device_id=(g, flipped(1 << bit)),
            device_id_type=MESH,
        )

    def send(*key):
        hop(*key).start()
        sent.append(key)

    def need(*key):
        if key not in arrived:
            arrived.add(key)
            hop(*key).wait_recv()

    def gather_start(stage, ch, parts=(0, 1), halves=(0, 1)):
        for place in range(bits):
            for p in parts:
                for half in halves:
                    send(stage, ch, p, half, 1 << orders[half][place])

    def gather_forward(stage, ch, parts=(0, 1)):
        for step in range(1, bits):
            for p in parts:
                for half in range(2):
                    order = orders[half]
                    for mask in by_size:
                        if mask >> order[step - 1] & 1 and not any(
                            mask >> bit & 1 for bit in order[step:]
                        ):
                            need(stage, ch, p, half, mask)
                            for bit in order[step:]:
                                send(stage, ch, p, half, mask | 1 << bit)

    def gather_wait(stage, ch, mask):
        if mask:
            for p in range(2):
                for half in range(2):
                    need(stage, ch, p, half, mask)

    def slot(ch, p, index):
        return updates.at[ch, p, pl.ds(pl.multiple_of(index * border_rows, border_rows), border_rows), :]

    def right_copy(ch, p, s, origin):
        return pltpu.make_async_remote_copy(
            src_ref=slot(ch, p, origin),
            dst_ref=slot(ch, p, origin),
            send_sem=right_send.at[ch, p, s],
            recv_sem=right_recv.at[ch, p, s],
            device_id=(g + 2, b),
            device_id_type=MESH,
        )

    def left_copy(ch, p, s, origin):
        return pltpu.make_async_remote_copy(
            src_ref=slot(ch, p, origin),
            dst_ref=slot(ch, p, origin),
            send_sem=left_send.at[ch, p, s],
            recv_sem=left_recv.at[ch, p, s],
            device_id=(g - 2, b),
            device_id_type=MESH,
        )

    passed = set()

    def pass_on(ch, p, s):
        if s >= pairs or (ch, p, s) in passed:
            return
        passed.add((ch, p, s))

        @pl.when(k >= s)
        def _():
            if s:
                right_copy(ch, p, s - 1, k - s).wait_recv()

            @pl.when(has_right)
            def _():
                right_copy(ch, p, s, k - s).start()

        @pl.when(k + s < pairs)
        def _():
            if s:
                left_copy(ch, p, s - 1, k + s).wait_recv()

            @pl.when(has_left)
            def _():
                left_copy(ch, p, s, k + s).start()

    def pass_drain(ch, p, s):
        @pl.when((k >= s) & has_right)
        def _():
            right_copy(ch, p, s, k - s).wait_send()

        @pl.when((k + s < pairs) & has_left)
        def _():
            left_copy(ch, p, s, k + s).wait_send()

    def swap_copy(source, target, send_sem, recv_sem):
        return pltpu.make_async_remote_copy(
            src_ref=source,
            dst_ref=target,
            send_sem=send_sem,
            recv_sem=recv_sem,
            device_id=(partner, b),
            device_id_type=MESH,
        )

    def half_copy(ch, p):
        return swap_copy(half_out.at[ch, p], half_in.at[ch, p], h_send.at[ch, p], h_recv.at[ch, p])

    def last_copy(ch):
        return swap_copy(last_out.at[ch], last_in.at[ch], y_send.at[ch], y_recv.at[ch])

    def product(matrix, first, tile, stage, ch, origin):
        rows = buffers[stage].shape[2] // slots
        columns = pl.ds(pl.multiple_of(origin * rows, rows), rows)
        left = matrix[:, pl.ds(first, tile), columns].reshape(2 * tile, rows)
        block = jnp.concatenate(
            [shard(stage, ch, 0, origin)[...], shard(stage, ch, 1, origin)[...]], axis=1
        )
        value = jnp.dot(left, block, preferred_element_type=f32)
        return value.reshape(2, tile, 2 * LANES)

    def accumulate(matrix, sums, stage, ch, mask):
        gather_wait(stage, ch, mask)
        rows = matrix.shape[1]
        tile = tile_of(rows)
        origin = flipped(mask)

        @pl.loop(0, rows // tile)
        def _(i):
            first = pl.multiple_of(i * tile, tile)
            value = product(matrix, first, tile, stage, ch, origin)
            if mask:
                value = sums[:, pl.ds(first, tile), :] + value
            sums[:, pl.ds(first, tile), :] = value

    def finished(matrix, sums, stage, ch, first, tile):
        value = product(matrix, first, tile, stage, ch, flipped(slots - 1))
        if slots > 1:
            value = sums[:, pl.ds(first, tile), :] + value
        real_part = value[0, :, :LANES] - value[1, :, LANES:]
        imag_part = value[0, :, LANES:] + value[1, :, :LANES]
        return real_part, imag_part

    def solve_child(ch):
        gather_wait(0, ch, slots - 1)
        count = child_rows // 2
        tile = tile_of(count)
        for half in range(2):

            @pl.loop(0, count // tile)
            def _(i):
                first = pl.multiple_of(half * count + i * tile, tile)
                parts = finished(inverse, total, 0, ch, first, tile)
                place = pl.ds(pl.multiple_of(b * child_rows + first, tile), tile)
                for p in range(2):
                    gather_sol[ch, p, place, :] = parts[p].astype(bf16)

            gather_start(1, ch, halves=(half,))
        for p in range(2):
            child_store(ch, p).start()

    def make_updates(ch):
        gather_wait(1, ch, slots - 1)
        tile = tile_of(border_rows)

        @pl.loop(0, border_rows // tile)
        def _(i):
            first = pl.multiple_of(i * tile, tile)
            parts = finished(border, total, 1, ch, first, tile)
            place = pl.ds(pl.multiple_of(k * border_rows + first, tile), tile)
            for p in range(2):
                updates[ch, p, place, :] = (-parts[p]).astype(bf16)

        for p in range(2):
            pass_on(ch, p, 0)

    added = set()

    def add_from(ch, p, s):
        if (ch, p, s) in added:
            return
        added.add((ch, p, s))

        def add(origin):
            columns = pl.ds(pl.multiple_of(origin * border_rows, border_rows), border_rows)
            tile = tile_of(half_rows)

            @pl.loop(0, 2 * half_rows // tile)
            def _(i):
                here = pl.ds(pl.multiple_of(i * tile, tile), tile)
                value = jnp.dot(
                    onehot[here, columns], slot(ch, p, origin)[...], preferred_element_type=f32
                )
                if s:
                    value = right_total[p, here, :] + value
                right_total[p, here, :] = value

        if s == 0:
            add(k)
            return

        @pl.when(k >= s)
        def _():
            add(k - s)

        @pl.when(k + s < pairs)
        def _():
            add(k + s)

    def add_updates(ch, p):
        for s in range(pairs):
            add_from(ch, p, s)
        other = pl.ds(pl.multiple_of((1 - core) * half_rows, half_rows), half_rows)
        mine = pl.ds(pl.multiple_of(core * half_rows, half_rows), half_rows)
        half_out[ch, p] = right_total[p, other, :].astype(bf16)
        half_copy(ch, p).start()
        value = right_total[p, mine, :] + parent_rhs[p, :, pl.ds(ch * LANES, LANES)].astype(f32)
        half_copy(ch, p).wait_recv()
        value = value + half_in[ch, p].astype(f32)
        shard(2, ch, p, b)[...] = value.astype(bf16)
        gather_start(2, ch, parts=(p,))

    def solve_parent(ch):
        gather_wait(2, ch, slots - 1)
        tile = tile_of(out_rows)

        @pl.loop(0, out_rows // tile)
        def _(i):
            first = pl.multiple_of((1 - core) * out_rows + i * tile, tile)
            parts = finished(parent, parent_total, 2, ch, first, tile)
            here = pl.ds(pl.multiple_of(i * tile, tile), tile)
            for p in range(2):
                last_out[ch, p, here, :] = parts[p].astype(bf16)

        last_copy(ch).start()

        @pl.loop(0, out_rows // tile)
        def _(i):
            first = pl.multiple_of(core * out_rows + i * tile, tile)
            parts = finished(parent, parent_total, 2, ch, first, tile)
            here = pl.ds(pl.multiple_of(i * tile, tile), tile)
            for p in range(2):
                parent_total[p, here, :LANES] = parts[p]

        last_copy(ch).wait_recv()

        @pl.loop(0, out_rows // tile)
        def _(i):
            here = pl.ds(pl.multiple_of(i * tile, tile), tile)
            for p in range(2):
                value = parent_total[p, here, :LANES] + last_in[ch, p, here, :].astype(f32)
                result[p, here, pl.ds(ch * LANES, LANES)] = value.astype(bf16)

        parent_store(ch).start()

    def child_store(ch, p):
        return pltpu.make_async_copy(
            shard(1, ch, p, b),
            child_out.at[0, p, :, pl.ds(ch * LANES, LANES)],
            store_sem.at[ch * 2 + p],
        )

    def parent_store(ch):
        lanes = pl.ds(ch * LANES, LANES)
        return pltpu.make_async_copy(
            result.at[:, :, lanes], parent_out.at[0, :, :, lanes], store_sem.at[2 * chunks + ch]
        )

    def build_onehot():
        loads[0].wait()
        tile = tile_of(half_rows)
        for other in range(pairs):
            group = 2 * other + core
            mine = owner[parent_of[group]] == k
            wanted = jnp.where(mine, row_map[pl.ds(group, 1), :], -1)

            @pl.loop(0, 2 * half_rows // tile)
            def _(i):
                first = i * tile
                base = (
                    lax.div(first, half_rows) * half_order
                    + b * half_rows
                    + lax.rem(first, half_rows)
                )
                rows = base + lax.broadcasted_iota(jnp.int32, (tile, border_rows), 0)
                hits = jnp.where(rows == wanted, 1.0, 0.0).astype(bf16)
                onehot[
                    pl.ds(pl.multiple_of(first, tile), tile),
                    other * border_rows : (other + 1) * border_rows,
                ] = hits

    gather_start(0, 0)
    for ch in range(chunks):
        gather_forward(0, ch)
        own_copies[2 * ch].wait()
        own_copies[2 * ch + 1].wait()
        if ch == 0:
            loads[1].wait()
        for mask in by_size[:-1]:
            accumulate(inverse, total, 0, ch, mask)
        if ch:
            for p in range(2):
                pass_on(ch - 1, p, 1)
        solve_child(ch)
        gather_forward(1, ch)
        if ch == 0:
            build_onehot()
            loads[2].wait()
        else:
            for p in range(2):
                pass_on(ch - 1, p, 2)
        for mask in by_size[:-1]:
            accumulate(border, total, 1, ch, mask)
        if ch + 1 < chunks:
            gather_start(0, ch + 1)
        make_updates(ch)
        if ch == 0:
            loads[3].wait()
            loads[4].wait()
            continue
        for s in range(3, pairs):
            for p in range(2):
                pass_on(ch - 1, p, s)
        for p in range(2):
            add_updates(ch - 1, p)
        gather_forward(2, ch - 1)
        for p in range(2):
            pass_on(ch, p, 1)
        for mask in by_size[:-1]:
            accumulate(parent, parent_total, 2, ch - 1, mask)
        solve_parent(ch - 1)
    ch = chunks - 1
    for s in range(1, pairs - 1):
        for p in range(2):
            pass_on(ch, p, s)
    for s in range(pairs - 1):
        for p in range(2):
            add_from(ch, p, s)
    for p in range(2):
        pass_on(ch, p, pairs - 1)
        add_updates(ch, p)
        gather_forward(2, ch, parts=(p,))
    for mask in by_size[:-1]:
        accumulate(parent, parent_total, 2, ch, mask)
    solve_parent(ch)
    for key in sent:
        hop(*key).wait_send()
    for ch in range(chunks):
        for p in range(2):
            for s in range(pairs - 1):
                pass_drain(ch, p, s)
            half_copy(ch, p).wait_send()
            child_store(ch, p).wait()
        last_copy(ch).wait_send()
        parent_store(ch).wait()


def per_device(
    slots,
    groups,
    child_inverse,
    border_block,
    child_rhs,
    parent_inverse,
    parent_rhs,
    parent_of,
    owner,
    row_map,
):
    sources = child_rhs.shape[3]
    chunks = sources // LANES
    pairs = groups // 2
    child_rows = child_inverse.shape[2]
    border_rows = border_block.shape[2]
    half_rows = parent_rhs.shape[2]
    out_rows = parent_inverse.shape[2] // 2
    bf16 = jnp.bfloat16
    dma = pltpu.SemaphoreType.DMA
    anywhere = pl.BlockSpec(memory_space=pl.ANY)
    scalars = pl.BlockSpec(memory_space=pltpu.SMEM)
    return pl.pallas_call(
        functools.partial(kernel, slots, groups),
        out_shape=(
            jax.ShapeDtypeStruct((1, 2, child_rows, sources), bf16),
            jax.ShapeDtypeStruct((1, 2, out_rows, sources), bf16),
        ),
        in_specs=[anywhere] * 5 + [scalars, scalars, anywhere],
        out_specs=(anywhere, anywhere),
        scratch_shapes=[
            pltpu.VMEM(child_inverse.shape[1:], bf16),
            pltpu.VMEM(border_block.shape[1:], bf16),
            pltpu.VMEM(parent_inverse.shape[1:], bf16),
            pltpu.VMEM(parent_rhs.shape[1:], bf16),
            pltpu.VMEM((groups, border_rows), jnp.int32),
            pltpu.VMEM((chunks, 2, slots * child_rows, LANES), bf16),
            pltpu.VMEM((chunks, 2, slots * child_rows, LANES), bf16),
            pltpu.VMEM((chunks, 2, slots * half_rows, LANES), bf16),
            pltpu.VMEM((chunks, 2, pairs * border_rows, LANES), bf16),
            pltpu.VMEM((2 * half_rows, pairs * border_rows), bf16),
            pltpu.VMEM((2, max(child_rows, border_rows), 2 * LANES), jnp.float32),
            pltpu.VMEM((2, 2 * out_rows, 2 * LANES), jnp.float32),
            pltpu.VMEM((2, 2 * half_rows, LANES), jnp.float32),
            pltpu.VMEM((chunks, 2, half_rows, LANES), bf16),
            pltpu.VMEM((chunks, 2, half_rows, LANES), bf16),
            pltpu.VMEM((chunks, 2, out_rows, LANES), bf16),
            pltpu.VMEM((chunks, 2, out_rows, LANES), bf16),
            pltpu.VMEM((2, out_rows, sources), bf16),
            dma((3, chunks, 2, 2, slots)),
            dma((3, chunks, 2, 2, slots)),
            dma((chunks, 2, pairs)),
            dma((chunks, 2, pairs)),
            dma((chunks, 2, pairs)),
            dma((chunks, 2, pairs)),
            dma((chunks, 2)),
            dma((chunks, 2)),
            dma((chunks,)),
            dma((chunks,)),
            dma((5,)),
            dma((2 * chunks,)),
            dma((3 * chunks,)),
        ],
        compiler_params=pltpu.CompilerParams(
            collective_id=0, has_side_effects=True, vmem_limit_bytes=56 * 1024 * 1024
        ),
    )(child_inverse, border_block, child_rhs, parent_inverse, parent_rhs, parent_of.reshape(-1), owner, row_map)


def solution(mesh):
    in_specs = (
        P("grp", None, "blk", None),
        P("grp", None, "blk", None),
        P("grp", None, "blk", None),
        P("grp", None, "blk", None),
        P("grp", None, "blk", None),
        P(),
        P(),
        P(),
    )
    out_specs = (P("grp", None, "blk", None), P("grp", None, "blk", None))
    return jax.shard_map(
        functools.partial(per_device, mesh.shape["blk"], mesh.shape["grp"]),
        mesh=mesh,
        in_specs=in_specs,
        out_specs=out_specs,
        check_vma=False,
    )
```

```python
import functools

import jax
import jax.numpy as jnp
from jax import lax
from jax.experimental import pallas as pl
from jax.experimental.pallas import tpu as pltpu
from jax.sharding import PartitionSpec as P

MESH = pl.DeviceIdType.MESH
LANES = 128


def tile_of(rows):
    return 256 if rows % 256 == 0 else rows


def kernel(
    slots,
    groups,
    inverse_hbm,
    border_hbm,
    rhs_hbm,
    parent_hbm,
    parent_rhs_hbm,
    parent_of,
    owner,
    row_map_hbm,
    child_out,
    parent_out,
    inverse,
    border,
    parent,
    parent_rhs,
    row_map,
    gather_rhs,
    gather_sol,
    gather_right,
    updates,
    onehot,
    total,
    parent_total,
    right_total,
    half_out,
    half_in,
    last_out,
    last_in,
    result,
    ag_send,
    ag_recv,
    right_send,
    right_recv,
    left_send,
    left_recv,
    h_send,
    h_recv,
    y_send,
    y_recv,
    load_sem,
    own_sem,
    store_sem,
):
    pairs = groups // 2
    g = lax.axis_index("grp")
    b = lax.axis_index("blk")
    core = lax.rem(g, 2)
    k = lax.div(g, 2)
    chunks = gather_rhs.shape[0]
    bits = slots.bit_length() - 1
    child_rows = inverse.shape[1]
    border_rows = border.shape[1]
    half_rows = parent_rhs.shape[1]
    half_order = parent.shape[2]
    out_rows = result.shape[1]
    bf16 = jnp.bfloat16
    f32 = jnp.float32

    def flipped(mask):
        index = b
        for bit in range(bits):
            if mask >> bit & 1:
                index = index + (1 << bit) * (1 - 2 * lax.rem(lax.div(index, 1 << bit), 2))
        return index

    partner = g + 1 - 2 * core
    has_left = k > 0
    has_right = k < pairs - 1

    loads = [
        pltpu.make_async_copy(src, dst, load_sem.at[i])
        for i, (src, dst) in enumerate(
            [
                (row_map_hbm.at[:, pl.ds(pl.multiple_of(b * border_rows, LANES), border_rows)], row_map),
                (inverse_hbm.at[0], inverse),
                (border_hbm.at[0], border),
                (parent_rhs_hbm.at[0], parent_rhs),
                (parent_hbm.at[0], parent),
            ]
        )
    ]
    own_copies = [
        pltpu.make_async_copy(
            rhs_hbm.at[0, p, :, pl.ds(ch * LANES, LANES)],
            gather_rhs.at[ch, p, pl.ds(pl.multiple_of(b * child_rows, child_rows), child_rows), :],
            own_sem.at[ch * 2 + p],
        )
        for ch in range(chunks)
        for p in range(2)
    ]

    barrier = pltpu.get_barrier_semaphore()
    for bit in range(bits):
        pl.semaphore_signal(barrier, inc=1, device_id=(g, flipped(1 << bit)), device_id_type=MESH)
    pl.semaphore_signal(barrier, inc=1, device_id=(partner, b), device_id_type=MESH)

    @pl.when(has_left)
    def _():
        pl.semaphore_signal(barrier, inc=1, device_id=(g - 2, b), device_id_type=MESH)

    @pl.when(has_right)
    def _():
        pl.semaphore_signal(barrier, inc=1, device_id=(g + 2, b), device_id_type=MESH)

    neighbours = bits + 1 + jnp.where(has_left, 1, 0) + jnp.where(has_right, 1, 0)
    pl.semaphore_wait(barrier, neighbours)

    orders = (tuple(range(bits)), tuple(reversed(range(bits))))
    buffers = (gather_rhs, gather_sol, gather_right)
    arrived = set()
    sent = []
    by_size = sorted(range(slots), key=lambda mask: (mask.bit_count(), mask))

    def shard(stage, ch, p, index, half=None):
        rows = buffers[stage].shape[2] // slots
        count = rows if half is None else rows // 2
        first = pl.multiple_of(index * rows, rows)
        if half:
            first = pl.multiple_of(first + count, count)
        return buffers[stage].at[ch, p, pl.ds(first, count), :]

    def hop(stage, ch, p, half, mask):
        bit = [one for one in orders[half] if mask >> one & 1][-1]
        held = mask & ~(1 << bit)
        place = shard(stage, ch, p, flipped(held), half)
        source = place
        if stage == 0 and held == 0:
            count = child_rows // 2
            source = rhs_hbm.at[0, p, pl.ds(half * count, count), pl.ds(ch * LANES, LANES)]
        return pltpu.make_async_remote_copy(
            src_ref=source,
            dst_ref=place,
            send_sem=ag_send.at[stage, ch, p, half, mask],
            recv_sem=ag_recv.at[stage, ch, p, half, mask],
            device_id=(g, flipped(1 << bit)),
            device_id_type=MESH,
        )

    def send(*key):
        hop(*key).start()
        sent.append(key)

    def need(*key):
        if key not in arrived:
            arrived.add(key)
            hop(*key).wait_recv()

    def gather_start(stage, ch, parts=(0, 1), halves=(0, 1)):
        for place in range(bits):
            for p in parts:
                for half in halves:
                    send(stage, ch, p, half, 1 << orders[half][place])

    def gather_forward(stage, ch, parts=(0, 1)):
        for step in range(1, bits):
            for p in parts:
                for half in range(2):
                    order = orders[half]
                    for mask in by_size:
                        if mask >> order[step - 1] & 1 and not any(
                            mask >> bit & 1 for bit in order[step:]
                        ):
                            need(stage, ch, p, half, mask)
                            for bit in order[step:]:
                                send(stage, ch, p, half, mask | 1 << bit)

    def gather_wait(stage, ch, mask):
        if mask:
            for p in range(2):
                for half in range(2):
                    need(stage, ch, p, half, mask)

    def slot(ch, p, index):
        return updates.at[ch, p, pl.ds(pl.multiple_of(index * border_rows, border_rows), border_rows), :]

    def right_copy(ch, p, s, origin):
        return pltpu.make_async_remote_copy(
            src_ref=slot(ch, p, origin),
            dst_ref=slot(ch, p, origin),
            send_sem=right_send.at[ch, p, s],
            recv_sem=right_recv.at[ch, p, s],
            device_id=(g + 2, b),
            device_id_type=MESH,
        )

    def left_copy(ch, p, s, origin):
        return pltpu.make_async_remote_copy(
            src_ref=slot(ch, p, origin),
            dst_ref=slot(ch, p, origin),
            send_sem=left_send.at[ch, p, s],
            recv_sem=left_recv.at[ch, p, s],
            device_id=(g - 2, b),
            device_id_type=MESH,
        )

    passed = set()

    def pass_on(ch, p, s):
        if s >= pairs or (ch, p, s) in passed:
            return
        passed.add((ch, p, s))

        @pl.when(k >= s)
        def _():
            if s:
                right_copy(ch, p, s - 1, k - s).wait_recv()

            @pl.when(has_right)
            def _():
                right_copy(ch, p, s, k - s).start()

        @pl.when(k + s < pairs)
        def _():
            if s:
                left_copy(ch, p, s - 1, k + s).wait_recv()

            @pl.when(has_left)
            def _():
                left_copy(ch, p, s, k + s).start()

    def pass_drain(ch, p, s):
        @pl.when((k >= s) & has_right)
        def _():
            right_copy(ch, p, s, k - s).wait_send()

        @pl.when((k + s < pairs) & has_left)
        def _():
            left_copy(ch, p, s, k + s).wait_send()

    def swap_copy(source, target, send_sem, recv_sem):
        return pltpu.make_async_remote_copy(
            src_ref=source,
            dst_ref=target,
            send_sem=send_sem,
            recv_sem=recv_sem,
            device_id=(partner, b),
            device_id_type=MESH,
        )

    def half_copy(ch, p):
        return swap_copy(half_out.at[ch, p], half_in.at[ch, p], h_send.at[ch, p], h_recv.at[ch, p])

    def last_copy(ch):
        return swap_copy(last_out.at[ch], last_in.at[ch], y_send.at[ch], y_recv.at[ch])

    def product(matrix, first, tile, stage, ch, origin):
        rows = buffers[stage].shape[2] // slots
        columns = pl.ds(pl.multiple_of(origin * rows, rows), rows)
        left = matrix[:, pl.ds(first, tile), columns].reshape(2 * tile, rows)
        block = jnp.concatenate(
            [shard(stage, ch, 0, origin)[...], shard(stage, ch, 1, origin)[...]], axis=1
        )
        value = jnp.dot(left, block, preferred_element_type=f32)
        return value.reshape(2, tile, 2 * LANES)

    def accumulate(matrix, sums, stage, ch, mask):
        gather_wait(stage, ch, mask)
        rows = matrix.shape[1]
        tile = tile_of(rows)
        origin = flipped(mask)

        @pl.loop(0, rows // tile)
        def _(i):
            first = pl.multiple_of(i * tile, tile)
            value = product(matrix, first, tile, stage, ch, origin)
            if mask:
                value = sums[:, pl.ds(first, tile), :] + value
            sums[:, pl.ds(first, tile), :] = value

    def finished(matrix, sums, stage, ch, first, tile):
        value = product(matrix, first, tile, stage, ch, flipped(slots - 1))
        if slots > 1:
            value = sums[:, pl.ds(first, tile), :] + value
        real_part = value[0, :, :LANES] - value[1, :, LANES:]
        imag_part = value[0, :, LANES:] + value[1, :, :LANES]
        return real_part, imag_part

    def solve_child(ch):
        gather_wait(0, ch, slots - 1)
        count = child_rows // 2
        tile = tile_of(count)
        for half in range(2):

            @pl.loop(0, count // tile)
            def _(i):
                first = pl.multiple_of(half * count + i * tile, tile)
                parts = finished(inverse, total, 0, ch, first, tile)
                place = pl.ds(pl.multiple_of(b * child_rows + first, tile), tile)
                for p in range(2):
                    gather_sol[ch, p, place, :] = parts[p].astype(bf16)

            gather_start(1, ch, halves=(half,))
        for p in range(2):
            child_store(ch, p).start()

    def make_updates(ch):
        gather_wait(1, ch, slots - 1)
        tile = tile_of(border_rows)

        @pl.loop(0, border_rows // tile)
        def _(i):
            first = pl.multiple_of(i * tile, tile)
            parts = finished(border, total, 1, ch, first, tile)
            place = pl.ds(pl.multiple_of(k * border_rows + first, tile), tile)
            for p in range(2):
                updates[ch, p, place, :] = (-parts[p]).astype(bf16)

        for p in range(2):
            pass_on(ch, p, 0)

    added = set()

    def add_from(ch, p, s):
        if (ch, p, s) in added:
            return
        added.add((ch, p, s))

        def add(origin):
            columns = pl.ds(pl.multiple_of(origin * border_rows, border_rows), border_rows)
            tile = tile_of(half_rows)

            @pl.loop(0, 2 * half_rows // tile)
            def _(i):
                here = pl.ds(pl.multiple_of(i * tile, tile), tile)
                value = jnp.dot(
                    onehot[here, columns], slot(ch, p, origin)[...], preferred_element_type=f32
                )
                if s:
                    value = right_total[p, here, :] + value
                right_total[p, here, :] = value

        if s == 0:
            add(k)
            return

        @pl.when(k >= s)
        def _():
            add(k - s)

        @pl.when(k + s < pairs)
        def _():
            add(k + s)

    def add_updates(ch, p):
        for s in range(pairs):
            add_from(ch, p, s)
        other = pl.ds(pl.multiple_of((1 - core) * half_rows, half_rows), half_rows)
        mine = pl.ds(pl.multiple_of(core * half_rows, half_rows), half_rows)
        half_out[ch, p] = right_total[p, other, :].astype(bf16)
        half_copy(ch, p).start()
        value = right_total[p, mine, :] + parent_rhs[p, :, pl.ds(ch * LANES, LANES)].astype(f32)
        half_copy(ch, p).wait_recv()
        value = value + half_in[ch, p].astype(f32)
        shard(2, ch, p, b)[...] = value.astype(bf16)
        gather_start(2, ch, parts=(p,))

    def solve_parent(ch):
        gather_wait(2, ch, slots - 1)
        sums = parent_total.at[ch % 2]
        tile = tile_of(out_rows)

        @pl.loop(0, out_rows // tile)
        def _(i):
            first = pl.multiple_of((1 - core) * out_rows + i * tile, tile)
            parts = finished(parent, sums, 2, ch, first, tile)
            here = pl.ds(pl.multiple_of(i * tile, tile), tile)
            for p in range(2):
                last_out[ch, p, here, :] = parts[p].astype(bf16)

        last_copy(ch).start()

        @pl.loop(0, out_rows // tile)
        def _(i):
            first = pl.multiple_of(core * out_rows + i * tile, tile)
            parts = finished(parent, sums, 2, ch, first, tile)
            here = pl.ds(pl.multiple_of(i * tile, tile), tile)
            for p in range(2):
                sums[p, here, :LANES] = parts[p]

        last_copy(ch).wait_recv()

        @pl.loop(0, out_rows // tile)
        def _(i):
            here = pl.ds(pl.multiple_of(i * tile, tile), tile)
            for p in range(2):
                value = sums[p, here, :LANES] + last_in[ch, p, here, :].astype(f32)
                result[p, here, pl.ds(ch * LANES, LANES)] = value.astype(bf16)

        parent_store(ch).start()

    def child_store(ch, p):
        return pltpu.make_async_copy(
            shard(1, ch, p, b),
            child_out.at[0, p, :, pl.ds(ch * LANES, LANES)],
            store_sem.at[ch * 2 + p],
        )

    def parent_store(ch):
        lanes = pl.ds(ch * LANES, LANES)
        return pltpu.make_async_copy(
            result.at[:, :, lanes], parent_out.at[0, :, :, lanes], store_sem.at[2 * chunks + ch]
        )

    def build_onehot():
        loads[0].wait()
        tile = tile_of(half_rows)
        for other in range(pairs):
            group = 2 * other + core
            mine = owner[parent_of[group]] == k
            wanted = jnp.where(mine, row_map[pl.ds(group, 1), :], -1)

            @pl.loop(0, 2 * half_rows // tile)
            def _(i):
                first = i * tile
                base = (
                    lax.div(first, half_rows) * half_order
                    + b * half_rows
                    + lax.rem(first, half_rows)
                )
                rows = base + lax.broadcasted_iota(jnp.int32, (tile, border_rows), 0)
                hits = jnp.where(rows == wanted, 1.0, 0.0).astype(bf16)
                onehot[
                    pl.ds(pl.multiple_of(first, tile), tile),
                    other * border_rows : (other + 1) * border_rows,
                ] = hits

    def sum_children(ch):
        for s in range(pairs - 1):
            for p in range(2):
                pass_on(ch, p, s)
                add_from(ch, p, s)

    gather_start(0, 0)
    for copy in own_copies[:2] + [loads[1]] + own_copies[2:]:
        copy.start()
    for ch in range(chunks):
        gather_forward(0, ch)
        if ch == 0:
            for i in (2, 0, 3, 4):
                loads[i].start()
            loads[1].wait()
        own_copies[2 * ch].wait()
        own_copies[2 * ch + 1].wait()
        for i, mask in enumerate(by_size[:-1]):
            accumulate(inverse, total, 0, ch, mask)
            if ch and 1 <= i <= 2:
                pass_on(ch - 1, i - 1, 1)
        solve_child(ch)
        if ch:
            pass_on(ch - 1, 0, 2)
        gather_forward(1, ch)
        if ch:
            pass_on(ch - 1, 1, 2)
        else:
            build_onehot()
            loads[2].wait()
        for mask in by_size[:-1]:
            accumulate(border, total, 1, ch, mask)
        if ch + 1 < chunks:
            gather_start(0, ch + 1)
        if ch:
            sum_children(ch - 1)
        make_updates(ch)
        if ch == 0:
            loads[3].wait()
            loads[4].wait()
            continue
        for p in range(2):
            pass_on(ch - 1, p, pairs - 1)
            add_updates(ch - 1, p)
            pass_on(ch, p, 1)
        gather_forward(2, ch - 1)
        pass_on(ch, 0, 2)
        for i, mask in enumerate(by_size[:-1]):
            accumulate(parent, parent_total.at[(ch - 1) % 2], 2, ch - 1, mask)
            if i == 1:
                pass_on(ch, 1, 2)
        if ch + 1 < chunks:
            solve_parent(ch - 1)
    ch = chunks - 1
    sum_children(ch)
    pass_on(ch, 0, pairs - 1)
    add_updates(ch, 0)
    if ch:
        solve_parent(ch - 1)
    gather_forward(2, ch, parts=(0,))
    pass_on(ch, 1, pairs - 1)
    add_updates(ch, 1)
    gather_forward(2, ch, parts=(1,))
    for mask in by_size[:-1]:
        accumulate(parent, parent_total.at[ch % 2], 2, ch, mask)
    solve_parent(ch)
    for key in sent:
        hop(*key).wait_send()
    for ch in range(chunks):
        for p in range(2):
            for s in range(pairs - 1):
                pass_drain(ch, p, s)
            half_copy(ch, p).wait_send()
            child_store(ch, p).wait()
        last_copy(ch).wait_send()
        parent_store(ch).wait()


def hand_out(*refs):
    count = (len(refs) - 1) // 2
    sem = refs[-1]
    copies = []
    for i in range(count):
        rows = refs[i].shape[2] // 2
        for p in range(2):
            for half in range(2):
                piece = (0, p, pl.ds(half * rows, rows), slice(None))
                copies.append(
                    pltpu.make_async_copy(
                        refs[i].at[piece], refs[count + i].at[piece], sem.at[len(copies)]
                    )
                )
    for copy in copies:
        copy.start()
    for copy in copies:
        copy.wait()


def per_device(
    slots,
    groups,
    child_inverse,
    border_block,
    child_rhs,
    parent_inverse,
    parent_rhs,
    parent_of,
    owner,
    row_map,
):
    sources = child_rhs.shape[3]
    chunks = sources // LANES
    pairs = groups // 2
    child_rows = child_inverse.shape[2]
    border_rows = border_block.shape[2]
    half_rows = parent_rhs.shape[2]
    out_rows = parent_inverse.shape[2] // 2
    bf16 = jnp.bfloat16
    dma = pltpu.SemaphoreType.DMA
    anywhere = pl.BlockSpec(memory_space=pl.ANY)
    scalars = pl.BlockSpec(memory_space=pltpu.SMEM)
    results = pl.pallas_call(
        functools.partial(kernel, slots, groups),
        out_shape=(
            jax.ShapeDtypeStruct((1, 2, child_rows, sources), bf16),
            jax.ShapeDtypeStruct((1, 2, out_rows, sources), bf16),
        ),
        in_specs=[anywhere] * 5 + [scalars, scalars, anywhere],
        out_specs=(anywhere, anywhere),
        scratch_shapes=[
            pltpu.VMEM(child_inverse.shape[1:], bf16),
            pltpu.VMEM(border_block.shape[1:], bf16),
            pltpu.VMEM(parent_inverse.shape[1:], bf16),
            pltpu.VMEM(parent_rhs.shape[1:], bf16),
            pltpu.VMEM((groups, border_rows), jnp.int32),
            pltpu.VMEM((chunks, 2, slots * child_rows, LANES), bf16),
            pltpu.VMEM((chunks, 2, slots * child_rows, LANES), bf16),
            pltpu.VMEM((chunks, 2, slots * half_rows, LANES), bf16),
            pltpu.VMEM((chunks, 2, pairs * border_rows, LANES), bf16),
            pltpu.VMEM((2 * half_rows, pairs * border_rows), bf16),
            pltpu.VMEM((2, max(child_rows, border_rows), 2 * LANES), jnp.float32),
            pltpu.VMEM((2, 2, 2 * out_rows, 2 * LANES), jnp.float32),
            pltpu.VMEM((2, 2 * half_rows, LANES), jnp.float32),
            pltpu.VMEM((chunks, 2, half_rows, LANES), bf16),
            pltpu.VMEM((chunks, 2, half_rows, LANES), bf16),
            pltpu.VMEM((chunks, 2, out_rows, LANES), bf16),
            pltpu.VMEM((chunks, 2, out_rows, LANES), bf16),
            pltpu.VMEM((2, out_rows, sources), bf16),
            dma((3, chunks, 2, 2, slots)),
            dma((3, chunks, 2, 2, slots)),
            dma((chunks, 2, pairs)),
            dma((chunks, 2, pairs)),
            dma((chunks, 2, pairs)),
            dma((chunks, 2, pairs)),
            dma((chunks, 2)),
            dma((chunks, 2)),
            dma((chunks,)),
            dma((chunks,)),
            dma((5,)),
            dma((2 * chunks,)),
            dma((3 * chunks,)),
        ],
        compiler_params=pltpu.CompilerParams(
            collective_id=0, has_side_effects=True, vmem_limit_bytes=56 * 1024 * 1024
        ),
    )(child_inverse, border_block, child_rhs, parent_inverse, parent_rhs, parent_of.reshape(-1), owner, row_map)
    return pl.pallas_call(
        hand_out,
        out_shape=tuple(jax.ShapeDtypeStruct(one.shape, bf16) for one in results),
        in_specs=[anywhere] * 2,
        out_specs=(anywhere, anywhere),
        scratch_shapes=[dma((8,))],
        compiler_params=pltpu.CompilerParams(vmem_limit_bytes=56 * 1024 * 1024),
    )(*results)


def solution(mesh):
    in_specs = (
        P("grp", None, "blk", None),
        P("grp", None, "blk", None),
        P("grp", None, "blk", None),
        P("grp", None, "blk", None),
        P("grp", None, "blk", None),
        P(),
        P(),
        P(),
    )
    out_specs = (P("grp", None, "blk", None), P("grp", None, "blk", None))
    return jax.shard_map(
        functools.partial(per_device, mesh.shape["blk"], mesh.shape["grp"]),
        mesh=mesh,
        in_specs=in_specs,
        out_specs=out_specs,
        check_vma=False,
    )
```

```python
import functools

import jax
import jax.numpy as jnp
from jax import lax
from jax.experimental import pallas as pl
from jax.experimental.pallas import tpu as pltpu
from jax.sharding import PartitionSpec as P

MESH = pl.DeviceIdType.MESH
LANES = 128


def tile_of(rows):
    return 256 if rows % 256 == 0 else rows


def kernel(
    slots,
    groups,
    inverse_hbm,
    border_hbm,
    rhs_hbm,
    parent_hbm,
    parent_rhs_hbm,
    parent_of,
    owner,
    row_map_hbm,
    child_out,
    parent_out,
    inverse,
    border,
    parent,
    parent_rhs,
    row_map,
    gather_rhs,
    gather_sol,
    gather_right,
    updates,
    onehot,
    total,
    parent_total,
    right_total,
    half_out,
    half_in,
    last_out,
    last_in,
    result,
    ag_send,
    ag_recv,
    right_send,
    right_recv,
    left_send,
    left_recv,
    h_send,
    h_recv,
    y_send,
    y_recv,
    load_sem,
    own_sem,
    store_sem,
):
    pairs = groups // 2
    g = lax.axis_index("grp")
    b = lax.axis_index("blk")
    core = lax.rem(g, 2)
    k = lax.div(g, 2)
    chunks = gather_rhs.shape[0]
    bits = slots.bit_length() - 1
    child_rows = inverse.shape[1]
    border_rows = border.shape[1]
    half_rows = parent_rhs.shape[1]
    half_order = parent.shape[2]
    out_rows = result.shape[1]
    bf16 = jnp.bfloat16
    f32 = jnp.float32

    def flipped(mask):
        index = b
        for bit in range(bits):
            if mask >> bit & 1:
                index = index + (1 << bit) * (1 - 2 * lax.rem(lax.div(index, 1 << bit), 2))
        return index

    partner = g + 1 - 2 * core
    has_left = k > 0
    has_right = k < pairs - 1

    loads = [
        pltpu.make_async_copy(src, dst, load_sem.at[i])
        for i, (src, dst) in enumerate(
            [
                (row_map_hbm.at[:, pl.ds(pl.multiple_of(b * border_rows, LANES), border_rows)], row_map),
                (inverse_hbm.at[0], inverse),
                (border_hbm.at[0], border),
                (parent_rhs_hbm.at[0], parent_rhs),
                (parent_hbm.at[0], parent),
            ]
        )
    ]
    own_copies = [
        pltpu.make_async_copy(
            rhs_hbm.at[0, p, :, pl.ds(ch * LANES, LANES)],
            gather_rhs.at[ch, p, pl.ds(pl.multiple_of(b * child_rows, child_rows), child_rows), :],
            own_sem.at[ch * 2 + p],
        )
        for ch in range(chunks)
        for p in range(2)
    ]

    barrier = pltpu.get_barrier_semaphore()
    for bit in range(bits):
        pl.semaphore_signal(barrier, inc=1, device_id=(g, flipped(1 << bit)), device_id_type=MESH)
    pl.semaphore_signal(barrier, inc=1, device_id=(partner, b), device_id_type=MESH)

    @pl.when(has_left)
    def _():
        pl.semaphore_signal(barrier, inc=1, device_id=(g - 2, b), device_id_type=MESH)

    @pl.when(has_right)
    def _():
        pl.semaphore_signal(barrier, inc=1, device_id=(g + 2, b), device_id_type=MESH)

    for copy in own_copies:
        copy.start()
    neighbours = bits + 1 + jnp.where(has_left, 1, 0) + jnp.where(has_right, 1, 0)
    pl.semaphore_wait(barrier, neighbours)

    orders = (tuple(range(bits)), tuple(reversed(range(bits))))
    buffers = (gather_rhs, gather_sol, gather_right)
    arrived = set()
    sent = []
    by_size = sorted(range(slots), key=lambda mask: (mask.bit_count(), mask))

    def shard(stage, ch, p, index, half=None):
        rows = buffers[stage].shape[2] // slots
        count = rows if half is None else rows // 2
        first = pl.multiple_of(index * rows, rows)
        if half:
            first = pl.multiple_of(first + count, count)
        return buffers[stage].at[ch, p, pl.ds(first, count), :]

    def hop(stage, ch, p, half, mask):
        bit = [one for one in orders[half] if mask >> one & 1][-1]
        held = mask & ~(1 << bit)
        place = shard(stage, ch, p, flipped(held), half)
        return pltpu.make_async_remote_copy(
            src_ref=place,
            dst_ref=place,
            send_sem=ag_send.at[stage, ch, p, half, mask],
            recv_sem=ag_recv.at[stage, ch, p, half, mask],
            device_id=(g, flipped(1 << bit)),
            device_id_type=MESH,
        )

    def send(*key):
        hop(*key).start()
        sent.append(key)

    def need(*key):
        if key not in arrived:
            arrived.add(key)
            hop(*key).wait_recv()

    def gather_start(stage, ch, parts=(0, 1), halves=(0, 1)):
        for place in range(bits):
            for p in parts:
                for half in halves:
                    send(stage, ch, p, half, 1 << orders[half][place])

    def gather_forward(stage, ch, parts=(0, 1)):
        for step in range(1, bits):
            for p in parts:
                for half in range(2):
                    order = orders[half]
                    for mask in by_size:
                        if mask >> order[step - 1] & 1 and not any(
                            mask >> bit & 1 for bit in order[step:]
                        ):
                            need(stage, ch, p, half, mask)
                            for bit in order[step:]:
                                send(stage, ch, p, half, mask | 1 << bit)

    def gather_wait(stage, ch, mask):
        if mask:
            for p in range(2):
                for half in range(2):
                    need(stage, ch, p, half, mask)

    def slot(ch, p, index):
        return updates.at[ch, p, pl.ds(pl.multiple_of(index * border_rows, border_rows), border_rows), :]

    def right_copy(ch, p, s, origin):
        return pltpu.make_async_remote_copy(
            src_ref=slot(ch, p, origin),
            dst_ref=slot(ch, p, origin),
            send_sem=right_send.at[ch, p, s],
            recv_sem=right_recv.at[ch, p, s],
            device_id=(g + 2, b),
            device_id_type=MESH,
        )

    def left_copy(ch, p, s, origin):
        return pltpu.make_async_remote_copy(
            src_ref=slot(ch, p, origin),
            dst_ref=slot(ch, p, origin),
            send_sem=left_send.at[ch, p, s],
            recv_sem=left_recv.at[ch, p, s],
            device_id=(g - 2, b),
            device_id_type=MESH,
        )

    passed = set()

    def pass_on(ch, p, s):
        if s >= pairs or (ch, p, s) in passed:
            return
        passed.add((ch, p, s))

        @pl.when(k >= s)
        def _():
            if s:
                right_copy(ch, p, s - 1, k - s).wait_recv()

            @pl.when(has_right)
            def _():
                right_copy(ch, p, s, k - s).start()

        @pl.when(k + s < pairs)
        def _():
            if s:
                left_copy(ch, p, s - 1, k + s).wait_recv()

            @pl.when(has_left)
            def _():
                left_copy(ch, p, s, k + s).start()

    def pass_drain(ch, p, s):
        @pl.when((k >= s) & has_right)
        def _():
            right_copy(ch, p, s, k - s).wait_send()

        @pl.when((k + s < pairs) & has_left)
        def _():
            left_copy(ch, p, s, k + s).wait_send()

    def swap_copy(source, target, send_sem, recv_sem):
        return pltpu.make_async_remote_copy(
            src_ref=source,
            dst_ref=target,
            send_sem=send_sem,
            recv_sem=recv_sem,
            device_id=(partner, b),
            device_id_type=MESH,
        )

    def half_copy(ch, p):
        return swap_copy(half_out.at[ch, p], half_in.at[ch, p], h_send.at[ch, p], h_recv.at[ch, p])

    def last_copy(ch):
        return swap_copy(last_out.at[ch], last_in.at[ch], y_send.at[ch], y_recv.at[ch])

    def product(matrix, first, tile, stage, ch, origin):
        rows = buffers[stage].shape[2] // slots
        columns = pl.ds(pl.multiple_of(origin * rows, rows), rows)
        left = matrix[:, pl.ds(first, tile), columns].reshape(2 * tile, rows)
        block = jnp.concatenate(
            [shard(stage, ch, 0, origin)[...], shard(stage, ch, 1, origin)[...]], axis=1
        )
        value = jnp.dot(left, block, preferred_element_type=f32)
        return value.reshape(2, tile, 2 * LANES)

    def accumulate(matrix, sums, stage, ch, mask):
        gather_wait(stage, ch, mask)
        rows = matrix.shape[1]
        tile = tile_of(rows)
        origin = flipped(mask)

        @pl.loop(0, rows // tile)
        def _(i):
            first = pl.multiple_of(i * tile, tile)
            value = product(matrix, first, tile, stage, ch, origin)
            if mask:
                value = sums[:, pl.ds(first, tile), :] + value
            sums[:, pl.ds(first, tile), :] = value

    def finished(matrix, sums, stage, ch, first, tile):
        value = product(matrix, first, tile, stage, ch, flipped(slots - 1))
        if slots > 1:
            value = sums[:, pl.ds(first, tile), :] + value
        real_part = value[0, :, :LANES] - value[1, :, LANES:]
        imag_part = value[0, :, LANES:] + value[1, :, :LANES]
        return real_part, imag_part

    def solve_child(ch):
        gather_wait(0, ch, slots - 1)
        count = child_rows // 2
        tile = tile_of(count)
        for half in range(2):

            @pl.loop(0, count // tile)
            def _(i):
                first = pl.multiple_of(half * count + i * tile, tile)
                parts = finished(inverse, total, 0, ch, first, tile)
                place = pl.ds(pl.multiple_of(b * child_rows + first, tile), tile)
                for p in range(2):
                    gather_sol[ch, p, place, :] = parts[p].astype(bf16)

            gather_start(1, ch, halves=(half,))
        for p in range(2):
            child_store(ch, p).start()

    def make_updates(ch):
        gather_wait(1, ch, slots - 1)
        tile = tile_of(border_rows)

        @pl.loop(0, border_rows // tile)
        def _(i):
            first = pl.multiple_of(i * tile, tile)
            parts = finished(border, total, 1, ch, first, tile)
            place = pl.ds(pl.multiple_of(k * border_rows + first, tile), tile)
            for p in range(2):
                updates[ch, p, place, :] = (-parts[p]).astype(bf16)

        for p in range(2):
            pass_on(ch, p, 0)

    added = set()

    def add_from(ch, p, s):
        if (ch, p, s) in added:
            return
        added.add((ch, p, s))

        def add(origin):
            columns = pl.ds(pl.multiple_of(origin * border_rows, border_rows), border_rows)
            tile = tile_of(half_rows)

            @pl.loop(0, 2 * half_rows // tile)
            def _(i):
                here = pl.ds(pl.multiple_of(i * tile, tile), tile)
                value = jnp.dot(
                    onehot[here, columns], slot(ch, p, origin)[...], preferred_element_type=f32
                )
                if s:
                    value = right_total[p, here, :] + value
                right_total[p, here, :] = value

        if s == 0:
            add(k)
            return

        @pl.when(k >= s)
        def _():
            add(k - s)

        @pl.when(k + s < pairs)
        def _():
            add(k + s)

    def add_updates(ch, p):
        for s in range(pairs):
            add_from(ch, p, s)
        other = pl.ds(pl.multiple_of((1 - core) * half_rows, half_rows), half_rows)
        mine = pl.ds(pl.multiple_of(core * half_rows, half_rows), half_rows)
        half_out[ch, p] = right_total[p, other, :].astype(bf16)
        half_copy(ch, p).start()
        value = right_total[p, mine, :] + parent_rhs[p, :, pl.ds(ch * LANES, LANES)].astype(f32)
        half_copy(ch, p).wait_recv()
        value = value + half_in[ch, p].astype(f32)
        shard(2, ch, p, b)[...] = value.astype(bf16)
        gather_start(2, ch, parts=(p,))

    def solve_parent(ch):
        gather_wait(2, ch, slots - 1)
        sums = parent_total.at[ch % 2]
        tile = tile_of(out_rows)

        @pl.loop(0, out_rows // tile)
        def _(i):
            first = pl.multiple_of((1 - core) * out_rows + i * tile, tile)
            parts = finished(parent, sums, 2, ch, first, tile)
            here = pl.ds(pl.multiple_of(i * tile, tile), tile)
            for p in range(2):
                last_out[ch, p, here, :] = parts[p].astype(bf16)

        last_copy(ch).start()

        @pl.loop(0, out_rows // tile)
        def _(i):
            first = pl.multiple_of(core * out_rows + i * tile, tile)
            parts = finished(parent, sums, 2, ch, first, tile)
            here = pl.ds(pl.multiple_of(i * tile, tile), tile)
            for p in range(2):
                sums[p, here, :LANES] = parts[p]

        last_copy(ch).wait_recv()

        @pl.loop(0, out_rows // tile)
        def _(i):
            here = pl.ds(pl.multiple_of(i * tile, tile), tile)
            for p in range(2):
                value = sums[p, here, :LANES] + last_in[ch, p, here, :].astype(f32)
                result[p, here, pl.ds(ch * LANES, LANES)] = value.astype(bf16)

        parent_store(ch).start()

    def child_store(ch, p):
        return pltpu.make_async_copy(
            shard(1, ch, p, b),
            child_out.at[0, p, :, pl.ds(ch * LANES, LANES)],
            store_sem.at[ch * 2 + p],
        )

    def parent_store(ch):
        lanes = pl.ds(ch * LANES, LANES)
        return pltpu.make_async_copy(
            result.at[:, :, lanes], parent_out.at[0, :, :, lanes], store_sem.at[2 * chunks + ch]
        )

    def build_onehot():
        loads[0].wait()
        tile = tile_of(half_rows)
        for other in range(pairs):
            group = 2 * other + core
            mine = owner[parent_of[group]] == k
            wanted = jnp.where(mine, row_map[pl.ds(group, 1), :], -1)

            @pl.loop(0, 2 * half_rows // tile)
            def _(i):
                first = i * tile
                base = (
                    lax.div(first, half_rows) * half_order
                    + b * half_rows
                    + lax.rem(first, half_rows)
                )
                rows = base + lax.broadcasted_iota(jnp.int32, (tile, border_rows), 0)
                hits = jnp.where(rows == wanted, 1.0, 0.0).astype(bf16)
                onehot[
                    pl.ds(pl.multiple_of(first, tile), tile),
                    other * border_rows : (other + 1) * border_rows,
                ] = hits

    def sum_children(ch):
        for s in range(pairs - 1):
            for p in range(2):
                pass_on(ch, p, s)
                add_from(ch, p, s)

    def start_rhs(ch):
        own_copies[2 * ch].wait()
        own_copies[2 * ch + 1].wait()
        gather_start(0, ch)

    start_rhs(0)
    loads[1].start()
    gather_forward(0, 0)
    for i in (2, 0, 3, 4):
        loads[i].start()
    loads[1].wait()
    for ch in range(chunks):
        for i, mask in enumerate(by_size[:-1]):
            accumulate(inverse, total, 0, ch, mask)
            if ch and 1 <= i <= 2:
                pass_on(ch - 1, i - 1, 1)
        solve_child(ch)
        if ch + 1 < chunks:
            start_rhs(ch + 1)
        if ch:
            pass_on(ch - 1, 0, 2)
        gather_forward(1, ch)
        if ch:
            pass_on(ch - 1, 1, 2)
        else:
            build_onehot()
            loads[2].wait()
        for mask in by_size[:-1]:
            accumulate(border, total, 1, ch, mask)
        if ch + 1 < chunks:
            gather_forward(0, ch + 1)
        if ch:
            sum_children(ch - 1)
        make_updates(ch)
        if ch == 0:
            loads[3].wait()
            loads[4].wait()
            continue
        for p in range(2):
            pass_on(ch - 1, p, pairs - 1)
            add_updates(ch - 1, p)
            pass_on(ch, p, 1)
        gather_forward(2, ch - 1)
        pass_on(ch, 0, 2)
        for i, mask in enumerate(by_size[:-1]):
            accumulate(parent, parent_total.at[(ch - 1) % 2], 2, ch - 1, mask)
            if i == 1:
                pass_on(ch, 1, 2)
        if ch + 1 < chunks:
            solve_parent(ch - 1)
    ch = chunks - 1
    sum_children(ch)
    pass_on(ch, 0, pairs - 1)
    add_updates(ch, 0)
    if ch:
        solve_parent(ch - 1)
    gather_forward(2, ch, parts=(0,))
    pass_on(ch, 1, pairs - 1)
    add_updates(ch, 1)
    gather_forward(2, ch, parts=(1,))
    for mask in by_size[:-1]:
        accumulate(parent, parent_total.at[ch % 2], 2, ch, mask)
    solve_parent(ch)
    for key in sent:
        hop(*key).wait_send()
    for ch in range(chunks):
        for p in range(2):
            for s in range(pairs - 1):
                pass_drain(ch, p, s)
            half_copy(ch, p).wait_send()
            child_store(ch, p).wait()
        last_copy(ch).wait_send()
        parent_store(ch).wait()


def hand_out(first_in, second_in, first_out, second_out, held, in_sem, out_sem):
    steps = []
    for i, (source, target) in enumerate([(first_in, first_out), (second_in, second_out)]):
        for p in range(2):
            j = 2 * i + p
            place = held.at[j]
            steps.append(
                (
                    pltpu.make_async_copy(source.at[0, p], place, in_sem.at[j]),
                    pltpu.make_async_copy(place, target.at[0, p], out_sem.at[j]),
                )
            )
    for take, _ in steps:
        take.start()
    for take, give in steps:
        take.wait()
        give.start()
    for _, give in steps:
        give.wait()


def per_device(
    slots,
    groups,
    child_inverse,
    border_block,
    child_rhs,
    parent_inverse,
    parent_rhs,
    parent_of,
    owner,
    row_map,
):
    sources = child_rhs.shape[3]
    chunks = sources // LANES
    pairs = groups // 2
    child_rows = child_inverse.shape[2]
    border_rows = border_block.shape[2]
    half_rows = parent_rhs.shape[2]
    out_rows = parent_inverse.shape[2] // 2
    bf16 = jnp.bfloat16
    dma = pltpu.SemaphoreType.DMA
    anywhere = pl.BlockSpec(memory_space=pl.ANY)
    scalars = pl.BlockSpec(memory_space=pltpu.SMEM)
    results = pl.pallas_call(
        functools.partial(kernel, slots, groups),
        out_shape=(
            jax.ShapeDtypeStruct((1, 2, child_rows, sources), bf16),
            jax.ShapeDtypeStruct((1, 2, out_rows, sources), bf16),
        ),
        in_specs=[anywhere] * 5 + [scalars, scalars, anywhere],
        out_specs=(anywhere, anywhere),
        scratch_shapes=[
            pltpu.VMEM(child_inverse.shape[1:], bf16),
            pltpu.VMEM(border_block.shape[1:], bf16),
            pltpu.VMEM(parent_inverse.shape[1:], bf16),
            pltpu.VMEM(parent_rhs.shape[1:], bf16),
            pltpu.VMEM((groups, border_rows), jnp.int32),
            pltpu.VMEM((chunks, 2, slots * child_rows, LANES), bf16),
            pltpu.VMEM((chunks, 2, slots * child_rows, LANES), bf16),
            pltpu.VMEM((chunks, 2, slots * half_rows, LANES), bf16),
            pltpu.VMEM((chunks, 2, pairs * border_rows, LANES), bf16),
            pltpu.VMEM((2 * half_rows, pairs * border_rows), bf16),
            pltpu.VMEM((2, max(child_rows, border_rows), 2 * LANES), jnp.float32),
            pltpu.VMEM((2, 2, 2 * out_rows, 2 * LANES), jnp.float32),
            pltpu.VMEM((2, 2 * half_rows, LANES), jnp.float32),
            pltpu.VMEM((chunks, 2, half_rows, LANES), bf16),
            pltpu.VMEM((chunks, 2, half_rows, LANES), bf16),
            pltpu.VMEM((chunks, 2, out_rows, LANES), bf16),
            pltpu.VMEM((chunks, 2, out_rows, LANES), bf16),
            pltpu.VMEM((2, out_rows, sources), bf16),
            dma((3, chunks, 2, 2, slots)),
            dma((3, chunks, 2, 2, slots)),
            dma((chunks, 2, pairs)),
            dma((chunks, 2, pairs)),
            dma((chunks, 2, pairs)),
            dma((chunks, 2, pairs)),
            dma((chunks, 2)),
            dma((chunks, 2)),
            dma((chunks,)),
            dma((chunks,)),
            dma((5,)),
            dma((2 * chunks,)),
            dma((3 * chunks,)),
        ],
        compiler_params=pltpu.CompilerParams(
            collective_id=0, has_side_effects=True, vmem_limit_bytes=56 * 1024 * 1024
        ),
    )(child_inverse, border_block, child_rhs, parent_inverse, parent_rhs, parent_of.reshape(-1), owner, row_map)
    return pl.pallas_call(
        hand_out,
        out_shape=tuple(jax.ShapeDtypeStruct(one.shape, bf16) for one in results),
        in_specs=[anywhere] * 2,
        out_specs=(anywhere, anywhere),
        scratch_shapes=[pltpu.VMEM((4, child_rows, sources), bf16), dma((4,)), dma((4,))],
        compiler_params=pltpu.CompilerParams(vmem_limit_bytes=56 * 1024 * 1024),
    )(*results)


def solution(mesh):
    in_specs = (
        P("grp", None, "blk", None),
        P("grp", None, "blk", None),
        P("grp", None, "blk", None),
        P("grp", None, "blk", None),
        P("grp", None, "blk", None),
        P(),
        P(),
        P(),
    )
    out_specs = (P("grp", None, "blk", None), P("grp", None, "blk", None))
    return jax.shard_map(
        functools.partial(per_device, mesh.shape["blk"], mesh.shape["grp"]),
        mesh=mesh,
        in_specs=in_specs,
        out_specs=out_specs,
        check_vma=False,
    )
```

```python
import functools

import jax
import jax.numpy as jnp
from jax import lax
from jax.experimental import pallas as pl
from jax.experimental.pallas import tpu as pltpu
from jax.sharding import PartitionSpec as P

MESH = pl.DeviceIdType.MESH
LANES = 128


def tile_of(rows):
    return 256 if rows % 256 == 0 else rows


def kernel(
    slots,
    groups,
    inverse_hbm,
    border_hbm,
    rhs_hbm,
    parent_hbm,
    parent_rhs_hbm,
    parent_of,
    owner,
    row_map_hbm,
    child_out,
    parent_out,
    inverse,
    border,
    parent,
    parent_rhs,
    row_map,
    gather_rhs,
    gather_sol,
    gather_right,
    updates,
    onehot,
    total,
    parent_total,
    right_total,
    half_out,
    half_in,
    last_out,
    last_in,
    result,
    ag_send,
    ag_recv,
    right_send,
    right_recv,
    left_send,
    left_recv,
    h_send,
    h_recv,
    y_send,
    y_recv,
    load_sem,
    own_sem,
    store_sem,
):
    pairs = groups // 2
    g = lax.axis_index("grp")
    b = lax.axis_index("blk")
    core = lax.rem(g, 2)
    k = lax.div(g, 2)
    chunks = gather_rhs.shape[0]
    bits = slots.bit_length() - 1
    child_rows = inverse.shape[1]
    border_rows = border.shape[1]
    half_rows = parent_rhs.shape[1]
    half_order = parent.shape[2]
    out_rows = result.shape[1]
    bf16 = jnp.bfloat16
    f32 = jnp.float32

    def flipped(mask):
        index = b
        for bit in range(bits):
            if mask >> bit & 1:
                index = index + (1 << bit) * (1 - 2 * lax.rem(lax.div(index, 1 << bit), 2))
        return index

    partner = g + 1 - 2 * core
    has_left = k > 0
    has_right = k < pairs - 1

    loads = [
        pltpu.make_async_copy(src, dst, load_sem.at[i])
        for i, (src, dst) in enumerate(
            [
                (row_map_hbm.at[:, pl.ds(pl.multiple_of(b * border_rows, LANES), border_rows)], row_map),
                (inverse_hbm.at[0], inverse),
                (border_hbm.at[0], border),
                (parent_rhs_hbm.at[0], parent_rhs),
                (parent_hbm.at[0], parent),
            ]
        )
    ]
    own_copies = [
        pltpu.make_async_copy(
            rhs_hbm.at[0, p, :, pl.ds(ch * LANES, LANES)],
            gather_rhs.at[ch, p, pl.ds(pl.multiple_of(b * child_rows, child_rows), child_rows), :],
            own_sem.at[ch * 2 + p],
        )
        for ch in range(chunks)
        for p in range(2)
    ]

    barrier = pltpu.get_barrier_semaphore()
    for bit in range(bits):
        pl.semaphore_signal(barrier, inc=1, device_id=(g, flipped(1 << bit)), device_id_type=MESH)
    pl.semaphore_signal(barrier, inc=1, device_id=(partner, b), device_id_type=MESH)

    @pl.when(has_left)
    def _():
        pl.semaphore_signal(barrier, inc=1, device_id=(g - 2, b), device_id_type=MESH)

    @pl.when(has_right)
    def _():
        pl.semaphore_signal(barrier, inc=1, device_id=(g + 2, b), device_id_type=MESH)

    neighbours = bits + 1 + jnp.where(has_left, 1, 0) + jnp.where(has_right, 1, 0)
    pl.semaphore_wait(barrier, neighbours)

    orders = (tuple(range(bits)), tuple(reversed(range(bits))))
    buffers = (gather_rhs, gather_sol, gather_right)
    arrived = set()
    sent = []
    by_size = sorted(range(slots), key=lambda mask: (mask.bit_count(), mask))

    def shard(stage, ch, p, index, half=None):
        rows = buffers[stage].shape[2] // slots
        count = rows if half is None else rows // 2
        first = pl.multiple_of(index * rows, rows)
        if half:
            first = pl.multiple_of(first + count, count)
        return buffers[stage].at[ch, p, pl.ds(first, count), :]

    def hop(stage, ch, p, half, mask):
        bit = [one for one in orders[half] if mask >> one & 1][-1]
        held = mask & ~(1 << bit)
        place = shard(stage, ch, p, flipped(held), half)
        source = place
        if stage == 0 and held == 0:
            count = child_rows // 2
            source = rhs_hbm.at[0, p, pl.ds(half * count, count), pl.ds(ch * LANES, LANES)]
        return pltpu.make_async_remote_copy(
            src_ref=source,
            dst_ref=place,
            send_sem=ag_send.at[stage, ch, p, half, mask],
            recv_sem=ag_recv.at[stage, ch, p, half, mask],
            device_id=(g, flipped(1 << bit)),
            device_id_type=MESH,
        )

    def send(*key):
        hop(*key).start()
        sent.append(key)

    def need(*key):
        if key not in arrived:
            arrived.add(key)
            hop(*key).wait_recv()

    def gather_start(stage, ch, parts=(0, 1), halves=(0, 1)):
        for place in range(bits):
            for p in parts:
                for half in halves:
                    send(stage, ch, p, half, 1 << orders[half][place])

    def gather_forward(stage, ch, parts=(0, 1)):
        for step in range(1, bits):
            for p in parts:
                for half in range(2):
                    order = orders[half]
                    for mask in by_size:
                        if mask >> order[step - 1] & 1 and not any(
                            mask >> bit & 1 for bit in order[step:]
                        ):
                            need(stage, ch, p, half, mask)
                            for bit in order[step:]:
                                send(stage, ch, p, half, mask | 1 << bit)

    def gather_wait(stage, ch, mask):
        if mask:
            for p in range(2):
                for half in range(2):
                    need(stage, ch, p, half, mask)

    def slot(ch, p, index):
        return updates.at[ch, p, pl.ds(pl.multiple_of(index * border_rows, border_rows), border_rows), :]

    def right_copy(ch, p, s, origin):
        return pltpu.make_async_remote_copy(
            src_ref=slot(ch, p, origin),
            dst_ref=slot(ch, p, origin),
            send_sem=right_send.at[ch, p, s],
            recv_sem=right_recv.at[ch, p, s],
            device_id=(g + 2, b),
            device_id_type=MESH,
        )

    def left_copy(ch, p, s, origin):
        return pltpu.make_async_remote_copy(
            src_ref=slot(ch, p, origin),
            dst_ref=slot(ch, p, origin),
            send_sem=left_send.at[ch, p, s],
            recv_sem=left_recv.at[ch, p, s],
            device_id=(g - 2, b),
            device_id_type=MESH,
        )

    passed = set()

    def pass_on(ch, p, s):
        if s >= pairs or (ch, p, s) in passed:
            return
        passed.add((ch, p, s))

        @pl.when(k >= s)
        def _():
            if s:
                right_copy(ch, p, s - 1, k - s).wait_recv()

            @pl.when(has_right)
            def _():
                right_copy(ch, p, s, k - s).start()

        @pl.when(k + s < pairs)
        def _():
            if s:
                left_copy(ch, p, s - 1, k + s).wait_recv()

            @pl.when(has_left)
            def _():
                left_copy(ch, p, s, k + s).start()

    def pass_drain(ch, p, s):
        @pl.when((k >= s) & has_right)
        def _():
            right_copy(ch, p, s, k - s).wait_send()

        @pl.when((k + s < pairs) & has_left)
        def _():
            left_copy(ch, p, s, k + s).wait_send()

    def swap_copy(source, target, send_sem, recv_sem):
        return pltpu.make_async_remote_copy(
            src_ref=source,
            dst_ref=target,
            send_sem=send_sem,
            recv_sem=recv_sem,
            device_id=(partner, b),
            device_id_type=MESH,
        )

    def half_copy(ch, p):
        return swap_copy(half_out.at[ch, p], half_in.at[ch, p], h_send.at[ch, p], h_recv.at[ch, p])

    def last_copy(ch):
        return swap_copy(last_out.at[ch], last_in.at[ch], y_send.at[ch], y_recv.at[ch])

    def product(matrix, first, tile, stage, ch, origin):
        rows = buffers[stage].shape[2] // slots
        columns = pl.ds(pl.multiple_of(origin * rows, rows), rows)
        left = matrix[:, pl.ds(first, tile), columns].reshape(2 * tile, rows)
        block = jnp.concatenate(
            [shard(stage, ch, 0, origin)[...], shard(stage, ch, 1, origin)[...]], axis=1
        )
        value = jnp.dot(left, block, preferred_element_type=f32)
        return value.reshape(2, tile, 2 * LANES)

    def accumulate(matrix, sums, stage, ch, mask):
        gather_wait(stage, ch, mask)
        rows = matrix.shape[1]
        tile = tile_of(rows)
        origin = flipped(mask)

        @pl.loop(0, rows // tile)
        def _(i):
            first = pl.multiple_of(i * tile, tile)
            value = product(matrix, first, tile, stage, ch, origin)
            if mask:
                value = sums[:, pl.ds(first, tile), :] + value
            sums[:, pl.ds(first, tile), :] = value

    def finished(matrix, sums, stage, ch, first, tile):
        value = product(matrix, first, tile, stage, ch, flipped(slots - 1))
        if slots > 1:
            value = sums[:, pl.ds(first, tile), :] + value
        real_part = value[0, :, :LANES] - value[1, :, LANES:]
        imag_part = value[0, :, LANES:] + value[1, :, :LANES]
        return real_part, imag_part

    def solve_child(ch):
        gather_wait(0, ch, slots - 1)
        count = child_rows // 2
        tile = tile_of(count)
        for half in range(2):

            @pl.loop(0, count // tile)
            def _(i):
                first = pl.multiple_of(half * count + i * tile, tile)
                parts = finished(inverse, total, 0, ch, first, tile)
                place = pl.ds(pl.multiple_of(b * child_rows + first, tile), tile)
                for p in range(2):
                    gather_sol[ch, p, place, :] = parts[p].astype(bf16)

            gather_start(1, ch, halves=(half,))
        for p in range(2):
            child_store(ch, p).start()

    def make_updates(ch):
        gather_wait(1, ch, slots - 1)
        tile = tile_of(border_rows)

        @pl.loop(0, border_rows // tile)
        def _(i):
            first = pl.multiple_of(i * tile, tile)
            parts = finished(border, total, 1, ch, first, tile)
            place = pl.ds(pl.multiple_of(k * border_rows + first, tile), tile)
            for p in range(2):
                updates[ch, p, place, :] = (-parts[p]).astype(bf16)

        for p in range(2):
            pass_on(ch, p, 0)

    added = set()

    def add_from(ch, p, s):
        if (ch, p, s) in added:
            return
        added.add((ch, p, s))

        def add(origin):
            columns = pl.ds(pl.multiple_of(origin * border_rows, border_rows), border_rows)
            tile = 2 * half_rows

            @pl.loop(0, 2 * half_rows // tile)
            def _(i):
                here = pl.ds(pl.multiple_of(i * tile, tile), tile)
                value = jnp.dot(
                    onehot[here, columns], slot(ch, p, origin)[...], preferred_element_type=f32
                )
                if s:
                    value = right_total[p, here, :] + value
                right_total[p, here, :] = value

        if s == 0:
            add(k)
            return

        @pl.when(k >= s)
        def _():
            add(k - s)

        @pl.when(k + s < pairs)
        def _():
            add(k + s)

    def add_updates(ch, p):
        for s in range(pairs):
            add_from(ch, p, s)
        other = pl.ds(pl.multiple_of((1 - core) * half_rows, half_rows), half_rows)
        mine = pl.ds(pl.multiple_of(core * half_rows, half_rows), half_rows)
        half_out[ch, p] = right_total[p, other, :].astype(bf16)
        half_copy(ch, p).start()
        value = right_total[p, mine, :] + parent_rhs[p, :, pl.ds(ch * LANES, LANES)].astype(f32)
        half_copy(ch, p).wait_recv()
        value = value + half_in[ch, p].astype(f32)
        shard(2, ch, p, b)[...] = value.astype(bf16)
        gather_start(2, ch, parts=(p,))

    def solve_parent(ch):
        gather_wait(2, ch, slots - 1)
        sums = parent_total.at[ch % 2]
        tile = tile_of(out_rows)

        @pl.loop(0, out_rows // tile)
        def _(i):
            first = pl.multiple_of((1 - core) * out_rows + i * tile, tile)
            parts = finished(parent, sums, 2, ch, first, tile)
            here = pl.ds(pl.multiple_of(i * tile, tile), tile)
            for p in range(2):
                last_out[ch, p, here, :] = parts[p].astype(bf16)

        last_copy(ch).start()

        @pl.loop(0, out_rows // tile)
        def _(i):
            first = pl.multiple_of(core * out_rows + i * tile, tile)
            parts = finished(parent, sums, 2, ch, first, tile)
            here = pl.ds(pl.multiple_of(i * tile, tile), tile)
            for p in range(2):
                sums[p, here, :LANES] = parts[p]

        last_copy(ch).wait_recv()

        @pl.loop(0, out_rows // tile)
        def _(i):
            here = pl.ds(pl.multiple_of(i * tile, tile), tile)
            for p in range(2):
                value = sums[p, here, :LANES] + last_in[ch, p, here, :].astype(f32)
                result[p, here, pl.ds(ch * LANES, LANES)] = value.astype(bf16)

        parent_store(ch).start()

    def child_store(ch, p):
        return pltpu.make_async_copy(
            shard(1, ch, p, b),
            child_out.at[0, p, :, pl.ds(ch * LANES, LANES)],
            store_sem.at[ch * 2 + p],
        )

    def parent_store(ch):
        lanes = pl.ds(ch * LANES, LANES)
        return pltpu.make_async_copy(
            result.at[:, :, lanes], parent_out.at[0, :, :, lanes], store_sem.at[2 * chunks + ch]
        )

    def build_onehot():
        loads[0].wait()
        tile = tile_of(half_rows)
        for other in range(pairs):
            group = 2 * other + core
            mine = owner[parent_of[group]] == k
            wanted = jnp.where(mine, row_map[pl.ds(group, 1), :], -1)

            @pl.loop(0, 2 * half_rows // tile)
            def _(i):
                first = i * tile
                base = (
                    lax.div(first, half_rows) * half_order
                    + b * half_rows
                    + lax.rem(first, half_rows)
                )
                rows = base + lax.broadcasted_iota(jnp.int32, (tile, border_rows), 0)
                hits = jnp.where(rows == wanted, 1.0, 0.0).astype(bf16)
                onehot[
                    pl.ds(pl.multiple_of(first, tile), tile),
                    other * border_rows : (other + 1) * border_rows,
                ] = hits

    def sum_children(ch):
        for s in range(pairs - 1):
            for p in range(2):
                pass_on(ch, p, s)
                add_from(ch, p, s)

    gather_start(0, 0)
    for copy in own_copies[:2] + [loads[1]] + own_copies[2:]:
        copy.start()
    for ch in range(chunks):
        gather_forward(0, ch)
        if ch == 0:
            for i in (2, 0, 3, 4):
                loads[i].start()
            loads[1].wait()
        own_copies[2 * ch].wait()
        own_copies[2 * ch + 1].wait()
        for i, mask in enumerate(by_size[:-1]):
            accumulate(inverse, total, 0, ch, mask)
            if ch and 1 <= i <= 2:
                pass_on(ch - 1, i - 1, 1)
        solve_child(ch)
        if ch:
            pass_on(ch - 1, 0, 2)
        gather_forward(1, ch)
        if ch:
            pass_on(ch - 1, 1, 2)
        else:
            build_onehot()
            loads[2].wait()
        for mask in by_size[:-1]:
            accumulate(border, total, 1, ch, mask)
        if ch + 1 < chunks:
            gather_start(0, ch + 1)
        if ch:
            sum_children(ch - 1)
        make_updates(ch)
        if ch == 0:
            loads[3].wait()
            loads[4].wait()
            continue
        for p in range(2):
            pass_on(ch - 1, p, pairs - 1)
            add_updates(ch - 1, p)
            pass_on(ch, p, 1)
        gather_forward(2, ch - 1)
        pass_on(ch, 0, 2)
        for i, mask in enumerate(by_size[:-1]):
            accumulate(parent, parent_total.at[(ch - 1) % 2], 2, ch - 1, mask)
            if i == 1:
                pass_on(ch, 1, 2)
        if ch + 1 < chunks:
            solve_parent(ch - 1)
    ch = chunks - 1
    sum_children(ch)
    pass_on(ch, 0, pairs - 1)
    add_updates(ch, 0)
    if ch:
        solve_parent(ch - 1)
    gather_forward(2, ch, parts=(0,))
    pass_on(ch, 1, pairs - 1)
    add_updates(ch, 1)
    gather_forward(2, ch, parts=(1,))
    for mask in by_size[:-1]:
        accumulate(parent, parent_total.at[ch % 2], 2, ch, mask)
    solve_parent(ch)
    for key in sent:
        hop(*key).wait_send()
    for ch in range(chunks):
        for p in range(2):
            for s in range(pairs - 1):
                pass_drain(ch, p, s)
            half_copy(ch, p).wait_send()
            child_store(ch, p).wait()
        last_copy(ch).wait_send()
        parent_store(ch).wait()


def hand_out(first_in, second_in, first_out, second_out, held, in_sem, out_sem):
    steps = []
    for i, (source, target) in enumerate([(first_in, first_out), (second_in, second_out)]):
        for p in range(2):
            j = 2 * i + p
            place = held.at[j]
            steps.append(
                (
                    pltpu.make_async_copy(source.at[0, p], place, in_sem.at[j]),
                    pltpu.make_async_copy(place, target.at[0, p], out_sem.at[j]),
                )
            )
    for take, _ in steps:
        take.start()
    for take, give in steps:
        take.wait()
        give.start()
    for _, give in steps:
        give.wait()


def per_device(
    slots,
    groups,
    child_inverse,
    border_block,
    child_rhs,
    parent_inverse,
    parent_rhs,
    parent_of,
    owner,
    row_map,
):
    sources = child_rhs.shape[3]
    chunks = sources // LANES
    pairs = groups // 2
    child_rows = child_inverse.shape[2]
    border_rows = border_block.shape[2]
    half_rows = parent_rhs.shape[2]
    out_rows = parent_inverse.shape[2] // 2
    bf16 = jnp.bfloat16
    dma = pltpu.SemaphoreType.DMA
    anywhere = pl.BlockSpec(memory_space=pl.ANY)
    scalars = pl.BlockSpec(memory_space=pltpu.SMEM)
    results = pl.pallas_call(
        functools.partial(kernel, slots, groups),
        out_shape=(
            jax.ShapeDtypeStruct((1, 2, child_rows, sources), bf16),
            jax.ShapeDtypeStruct((1, 2, out_rows, sources), bf16),
        ),
        in_specs=[anywhere] * 5 + [scalars, scalars, anywhere],
        out_specs=(anywhere, anywhere),
        scratch_shapes=[
            pltpu.VMEM(child_inverse.shape[1:], bf16),
            pltpu.VMEM(border_block.shape[1:], bf16),
            pltpu.VMEM(parent_inverse.shape[1:], bf16),
            pltpu.VMEM(parent_rhs.shape[1:], bf16),
            pltpu.VMEM((groups, border_rows), jnp.int32),
            pltpu.VMEM((chunks, 2, slots * child_rows, LANES), bf16),
            pltpu.VMEM((chunks, 2, slots * child_rows, LANES), bf16),
            pltpu.VMEM((chunks, 2, slots * half_rows, LANES), bf16),
            pltpu.VMEM((chunks, 2, pairs * border_rows, LANES), bf16),
            pltpu.VMEM((2 * half_rows, pairs * border_rows), bf16),
            pltpu.VMEM((2, max(child_rows, border_rows), 2 * LANES), jnp.float32),
            pltpu.VMEM((2, 2, 2 * out_rows, 2 * LANES), jnp.float32),
            pltpu.VMEM((2, 2 * half_rows, LANES), jnp.float32),
            pltpu.VMEM((chunks, 2, half_rows, LANES), bf16),
            pltpu.VMEM((chunks, 2, half_rows, LANES), bf16),
            pltpu.VMEM((chunks, 2, out_rows, LANES), bf16),
            pltpu.VMEM((chunks, 2, out_rows, LANES), bf16),
            pltpu.VMEM((2, out_rows, sources), bf16),
            dma((3, chunks, 2, 2, slots)),
            dma((3, chunks, 2, 2, slots)),
            dma((chunks, 2, pairs)),
            dma((chunks, 2, pairs)),
            dma((chunks, 2, pairs)),
            dma((chunks, 2, pairs)),
            dma((chunks, 2)),
            dma((chunks, 2)),
            dma((chunks,)),
            dma((chunks,)),
            dma((5,)),
            dma((2 * chunks,)),
            dma((3 * chunks,)),
        ],
        compiler_params=pltpu.CompilerParams(
            collective_id=0, has_side_effects=True, vmem_limit_bytes=56 * 1024 * 1024
        ),
    )(child_inverse, border_block, child_rhs, parent_inverse, parent_rhs, parent_of.reshape(-1), owner, row_map)
    return pl.pallas_call(
        hand_out,
        out_shape=tuple(jax.ShapeDtypeStruct(one.shape, bf16) for one in results),
        in_specs=[anywhere] * 2,
        out_specs=(anywhere, anywhere),
        scratch_shapes=[pltpu.VMEM((4, child_rows, sources), bf16), dma((4,)), dma((4,))],
        compiler_params=pltpu.CompilerParams(vmem_limit_bytes=56 * 1024 * 1024),
    )(*results)


def solution(mesh):
    in_specs = (
        P("grp", None, "blk", None),
        P("grp", None, "blk", None),
        P("grp", None, "blk", None),
        P("grp", None, "blk", None),
        P("grp", None, "blk", None),
        P(),
        P(),
        P(),
    )
    out_specs = (P("grp", None, "blk", None), P("grp", None, "blk", None))
    return jax.shard_map(
        functools.partial(per_device, mesh.shape["blk"], mesh.shape["grp"]),
        mesh=mesh,
        in_specs=in_specs,
        out_specs=out_specs,
        check_vma=False,
    )
```

```python
import functools

import jax
import jax.numpy as jnp
from jax import lax
from jax.experimental import pallas as pl
from jax.experimental.pallas import tpu as pltpu
from jax.sharding import PartitionSpec as P

MESH = pl.DeviceIdType.MESH
LANES = 128


def tile_of(rows):
    return 512 if rows % 512 == 0 else rows


def kernel(
    slots,
    groups,
    inverse_hbm,
    border_hbm,
    rhs_hbm,
    parent_hbm,
    parent_rhs_hbm,
    parent_of,
    owner,
    row_map_hbm,
    child_out,
    parent_out,
    inverse,
    border,
    parent,
    parent_rhs,
    row_map,
    gather_rhs,
    gather_sol,
    gather_right,
    updates,
    onehot,
    total,
    parent_total,
    right_total,
    half_out,
    half_in,
    last_out,
    last_in,
    result,
    ag_send,
    ag_recv,
    right_send,
    right_recv,
    left_send,
    left_recv,
    h_send,
    h_recv,
    y_send,
    y_recv,
    load_sem,
    own_sem,
    store_sem,
):
    pairs = groups // 2
    g = lax.axis_index("grp")
    b = lax.axis_index("blk")
    core = lax.rem(g, 2)
    k = lax.div(g, 2)
    chunks = gather_rhs.shape[0]
    bits = slots.bit_length() - 1
    child_rows = inverse.shape[1]
    border_rows = border.shape[1]
    half_rows = parent_rhs.shape[1]
    half_order = parent.shape[2]
    out_rows = result.shape[1]
    bf16 = jnp.bfloat16
    f32 = jnp.float32

    def flipped(mask):
        index = b
        for bit in range(bits):
            if mask >> bit & 1:
                index = index + (1 << bit) * (1 - 2 * lax.rem(lax.div(index, 1 << bit), 2))
        return index

    partner = g + 1 - 2 * core
    has_left = k > 0
    has_right = k < pairs - 1

    loads = [
        pltpu.make_async_copy(src, dst, load_sem.at[i])
        for i, (src, dst) in enumerate(
            [
                (row_map_hbm.at[:, pl.ds(pl.multiple_of(b * border_rows, LANES), border_rows)], row_map),
                (inverse_hbm.at[0], inverse),
                (border_hbm.at[0], border),
                (parent_rhs_hbm.at[0], parent_rhs),
                (parent_hbm.at[0], parent),
            ]
        )
    ]
    own_copies = [
        pltpu.make_async_copy(
            rhs_hbm.at[0, p, :, pl.ds(ch * LANES, LANES)],
            gather_rhs.at[ch, p, pl.ds(pl.multiple_of(b * child_rows, child_rows), child_rows), :],
            own_sem.at[ch * 2 + p],
        )
        for ch in range(chunks)
        for p in range(2)
    ]

    barrier = pltpu.get_barrier_semaphore()
    for bit in range(bits):
        pl.semaphore_signal(barrier, inc=1, device_id=(g, flipped(1 << bit)), device_id_type=MESH)
    pl.semaphore_signal(barrier, inc=1, device_id=(partner, b), device_id_type=MESH)

    @pl.when(has_left)
    def _():
        pl.semaphore_signal(barrier, inc=1, device_id=(g - 2, b), device_id_type=MESH)

    @pl.when(has_right)
    def _():
        pl.semaphore_signal(barrier, inc=1, device_id=(g + 2, b), device_id_type=MESH)

    neighbours = bits + 1 + jnp.where(has_left, 1, 0) + jnp.where(has_right, 1, 0)
    pl.semaphore_wait(barrier, neighbours)

    orders = (tuple(range(bits)), tuple(reversed(range(bits))))
    buffers = (gather_rhs, gather_sol, gather_right)
    arrived = set()
    sent = []
    by_size = sorted(range(slots), key=lambda mask: (mask.bit_count(), mask))

    def shard(stage, ch, p, index, half=None):
        rows = buffers[stage].shape[2] // slots
        count = rows if half is None else rows // 2
        first = pl.multiple_of(index * rows, rows)
        if half:
            first = pl.multiple_of(first + count, count)
        return buffers[stage].at[ch, p, pl.ds(first, count), :]

    def hop(stage, ch, p, half, mask):
        bit = [one for one in orders[half] if mask >> one & 1][-1]
        held = mask & ~(1 << bit)
        place = shard(stage, ch, p, flipped(held), half)
        source = place
        if stage == 0 and held == 0:
            count = child_rows // 2
            source = rhs_hbm.at[0, p, pl.ds(half * count, count), pl.ds(ch * LANES, LANES)]
        return pltpu.make_async_remote_copy(
            src_ref=source,
            dst_ref=place,
            send_sem=ag_send.at[stage, ch, p, half, mask],
            recv_sem=ag_recv.at[stage, ch, p, half, mask],
            device_id=(g, flipped(1 << bit)),
            device_id_type=MESH,
        )

    def send(*key):
        hop(*key).start()
        sent.append(key)

    def need(*key):
        if key not in arrived:
            arrived.add(key)
            hop(*key).wait_recv()

    def gather_start(stage, ch, parts=(0, 1), halves=(0, 1)):
        for place in range(bits):
            for p in parts:
                for half in halves:
                    send(stage, ch, p, half, 1 << orders[half][place])

    def gather_forward(stage, ch, parts=(0, 1)):
        for step in range(1, bits):
            for p in parts:
                for half in range(2):
                    order = orders[half]
                    for mask in by_size:
                        if mask >> order[step - 1] & 1 and not any(
                            mask >> bit & 1 for bit in order[step:]
                        ):
                            need(stage, ch, p, half, mask)
                            for bit in order[step:]:
                                send(stage, ch, p, half, mask | 1 << bit)

    def gather_wait(stage, ch, mask):
        if mask:
            for p in range(2):
                for half in range(2):
                    need(stage, ch, p, half, mask)

    def slot(ch, p, index):
        return updates.at[ch, p, pl.ds(pl.multiple_of(index * border_rows, border_rows), border_rows), :]

    def right_copy(ch, p, s, origin):
        return pltpu.make_async_remote_copy(
            src_ref=slot(ch, p, origin),
            dst_ref=slot(ch, p, origin),
            send_sem=right_send.at[ch, p, s],
            recv_sem=right_recv.at[ch, p, s],
            device_id=(g + 2, b),
            device_id_type=MESH,
        )

    def left_copy(ch, p, s, origin):
        return pltpu.make_async_remote_copy(
            src_ref=slot(ch, p, origin),
            dst_ref=slot(ch, p, origin),
            send_sem=left_send.at[ch, p, s],
            recv_sem=left_recv.at[ch, p, s],
            device_id=(g - 2, b),
            device_id_type=MESH,
        )

    passed = set()

    def pass_on(ch, p, s):
        if s >= pairs or (ch, p, s) in passed:
            return
        passed.add((ch, p, s))

        @pl.when(k >= s)
        def _():
            if s:
                right_copy(ch, p, s - 1, k - s).wait_recv()

            @pl.when(has_right)
            def _():
                right_copy(ch, p, s, k - s).start()

        @pl.when(k + s < pairs)
        def _():
            if s:
                left_copy(ch, p, s - 1, k + s).wait_recv()

            @pl.when(has_left)
            def _():
                left_copy(ch, p, s, k + s).start()

    def pass_drain(ch, p, s):
        @pl.when((k >= s) & has_right)
        def _():
            right_copy(ch, p, s, k - s).wait_send()

        @pl.when((k + s < pairs) & has_left)
        def _():
            left_copy(ch, p, s, k + s).wait_send()

    def swap_copy(source, target, send_sem, recv_sem):
        return pltpu.make_async_remote_copy(
            src_ref=source,
            dst_ref=target,
            send_sem=send_sem,
            recv_sem=recv_sem,
            device_id=(partner, b),
            device_id_type=MESH,
        )

    def half_copy(ch, p):
        return swap_copy(half_out.at[ch, p], half_in.at[ch, p], h_send.at[ch, p], h_recv.at[ch, p])

    def last_copy(ch):
        return swap_copy(last_out.at[ch], last_in.at[ch], y_send.at[ch], y_recv.at[ch])

    def product(matrix, first, tile, stage, ch, origin):
        rows = buffers[stage].shape[2] // slots
        columns = pl.ds(pl.multiple_of(origin * rows, rows), rows)
        left = matrix[:, pl.ds(first, tile), columns].reshape(2 * tile, rows)
        block = jnp.concatenate(
            [shard(stage, ch, 0, origin)[...], shard(stage, ch, 1, origin)[...]], axis=1
        )
        value = jnp.dot(left, block, preferred_element_type=f32)
        return value.reshape(2, tile, 2 * LANES)

    def accumulate(matrix, sums, stage, ch, mask):
        gather_wait(stage, ch, mask)
        rows = matrix.shape[1]
        tile = tile_of(rows)
        origin = flipped(mask)

        @pl.loop(0, rows // tile)
        def _(i):
            first = pl.multiple_of(i * tile, tile)
            value = product(matrix, first, tile, stage, ch, origin)
            if mask:
                value = sums[:, pl.ds(first, tile), :] + value
            sums[:, pl.ds(first, tile), :] = value

    def finished(matrix, sums, stage, ch, first, tile):
        value = product(matrix, first, tile, stage, ch, flipped(slots - 1))
        if slots > 1:
            value = sums[:, pl.ds(first, tile), :] + value
        real_part = value[0, :, :LANES] - value[1, :, LANES:]
        imag_part = value[0, :, LANES:] + value[1, :, :LANES]
        return real_part, imag_part

    def solve_child(ch):
        gather_wait(0, ch, slots - 1)
        count = child_rows // 2
        tile = tile_of(count)
        for half in range(2):

            @pl.loop(0, count // tile)
            def _(i):
                first = pl.multiple_of(half * count + i * tile, tile)
                parts = finished(inverse, total, 0, ch, first, tile)
                place = pl.ds(pl.multiple_of(b * child_rows + first, tile), tile)
                for p in range(2):
                    gather_sol[ch, p, place, :] = parts[p].astype(bf16)

            gather_start(1, ch, halves=(half,))
        for p in range(2):
            child_store(ch, p).start()

    def make_updates(ch):
        gather_wait(1, ch, slots - 1)
        tile = tile_of(border_rows)

        @pl.loop(0, border_rows // tile)
        def _(i):
            first = pl.multiple_of(i * tile, tile)
            parts = finished(border, total, 1, ch, first, tile)
            place = pl.ds(pl.multiple_of(k * border_rows + first, tile), tile)
            for p in range(2):
                updates[ch, p, place, :] = (-parts[p]).astype(bf16)

        for p in range(2):
            pass_on(ch, p, 0)

    added = set()

    def add_from(ch, p, s):
        if (ch, p, s) in added:
            return
        added.add((ch, p, s))

        def add(origin):
            columns = pl.ds(pl.multiple_of(origin * border_rows, border_rows), border_rows)
            tile = 2 * half_rows

            @pl.loop(0, 2 * half_rows // tile)
            def _(i):
                here = pl.ds(pl.multiple_of(i * tile, tile), tile)
                value = jnp.dot(
                    onehot[here, columns], slot(ch, p, origin)[...], preferred_element_type=f32
                )
                if s:
                    value = right_total[p, here, :] + value
                right_total[p, here, :] = value

        if s == 0:
            add(k)
            return

        @pl.when(k >= s)
        def _():
            add(k - s)

        @pl.when(k + s < pairs)
        def _():
            add(k + s)

    def add_updates(ch, p):
        for s in range(pairs):
            add_from(ch, p, s)
        other = pl.ds(pl.multiple_of((1 - core) * half_rows, half_rows), half_rows)
        mine = pl.ds(pl.multiple_of(core * half_rows, half_rows), half_rows)
        half_out[ch, p] = right_total[p, other, :].astype(bf16)
        half_copy(ch, p).start()
        value = right_total[p, mine, :] + parent_rhs[p, :, pl.ds(ch * LANES, LANES)].astype(f32)
        half_copy(ch, p).wait_recv()
        value = value + half_in[ch, p].astype(f32)
        shard(2, ch, p, b)[...] = value.astype(bf16)
        gather_start(2, ch, parts=(p,))

    def solve_parent(ch):
        gather_wait(2, ch, slots - 1)
        sums = parent_total.at[ch % 2]
        tile = tile_of(out_rows)

        @pl.loop(0, out_rows // tile)
        def _(i):
            first = pl.multiple_of((1 - core) * out_rows + i * tile, tile)
            parts = finished(parent, sums, 2, ch, first, tile)
            here = pl.ds(pl.multiple_of(i * tile, tile), tile)
            for p in range(2):
                last_out[ch, p, here, :] = parts[p].astype(bf16)

        last_copy(ch).start()

        @pl.loop(0, out_rows // tile)
        def _(i):
            first = pl.multiple_of(core * out_rows + i * tile, tile)
            parts = finished(parent, sums, 2, ch, first, tile)
            here = pl.ds(pl.multiple_of(i * tile, tile), tile)
            for p in range(2):
                sums[p, here, :LANES] = parts[p]

        last_copy(ch).wait_recv()

        @pl.loop(0, out_rows // tile)
        def _(i):
            here = pl.ds(pl.multiple_of(i * tile, tile), tile)
            for p in range(2):
                value = sums[p, here, :LANES] + last_in[ch, p, here, :].astype(f32)
                result[p, here, pl.ds(ch * LANES, LANES)] = value.astype(bf16)

        parent_store(ch).start()

    def child_store(ch, p):
        return pltpu.make_async_copy(
            shard(1, ch, p, b),
            child_out.at[0, p, :, pl.ds(ch * LANES, LANES)],
            store_sem.at[ch * 2 + p],
        )

    def parent_store(ch):
        lanes = pl.ds(ch * LANES, LANES)
        return pltpu.make_async_copy(
            result.at[:, :, lanes], parent_out.at[0, :, :, lanes], store_sem.at[2 * chunks + ch]
        )

    def build_onehot():
        loads[0].wait()
        tile = tile_of(half_rows)
        for other in range(pairs):
            group = 2 * other + core
            mine = owner[parent_of[group]] == k
            wanted = jnp.where(mine, row_map[pl.ds(group, 1), :], -1)

            @pl.loop(0, 2 * half_rows // tile)
            def _(i):
                first = i * tile
                base = (
                    lax.div(first, half_rows) * half_order
                    + b * half_rows
                    + lax.rem(first, half_rows)
                )
                rows = base + lax.broadcasted_iota(jnp.int32, (tile, border_rows), 0)
                hits = jnp.where(rows == wanted, 1.0, 0.0).astype(bf16)
                onehot[
                    pl.ds(pl.multiple_of(first, tile), tile),
                    other * border_rows : (other + 1) * border_rows,
                ] = hits

    def sum_children(ch):
        for s in range(pairs - 1):
            for p in range(2):
                pass_on(ch, p, s)
                add_from(ch, p, s)

    gather_start(0, 0)
    for copy in own_copies[:2] + [loads[1]] + own_copies[2:]:
        copy.start()
    for ch in range(chunks):
        gather_forward(0, ch)
        if ch == 0:
            for i in (2, 0, 3, 4):
                loads[i].start()
            loads[1].wait()
        own_copies[2 * ch].wait()
        own_copies[2 * ch + 1].wait()
        for i, mask in enumerate(by_size[:-1]):
            accumulate(inverse, total, 0, ch, mask)
            if ch and 1 <= i <= 2:
                pass_on(ch - 1, i - 1, 1)
        solve_child(ch)
        if ch:
            pass_on(ch - 1, 0, 2)
        gather_forward(1, ch)
        if ch:
            pass_on(ch - 1, 1, 2)
        else:
            build_onehot()
            loads[2].wait()
        for mask in by_size[:-1]:
            accumulate(border, total, 1, ch, mask)
        if ch + 1 < chunks:
            gather_start(0, ch + 1)
        if ch:
            sum_children(ch - 1)
        make_updates(ch)
        if ch == 0:
            loads[3].wait()
            loads[4].wait()
            continue
        for p in range(2):
            pass_on(ch - 1, p, pairs - 1)
            add_updates(ch - 1, p)
            pass_on(ch, p, 1)
        gather_forward(2, ch - 1)
        pass_on(ch, 0, 2)
        for i, mask in enumerate(by_size[:-1]):
            accumulate(parent, parent_total.at[(ch - 1) % 2], 2, ch - 1, mask)
            if i == 1:
                pass_on(ch, 1, 2)
        if ch + 1 < chunks:
            solve_parent(ch - 1)
    ch = chunks - 1
    sum_children(ch)
    pass_on(ch, 0, pairs - 1)
    add_updates(ch, 0)
    if ch:
        solve_parent(ch - 1)
    gather_forward(2, ch, parts=(0,))
    pass_on(ch, 1, pairs - 1)
    add_updates(ch, 1)
    gather_forward(2, ch, parts=(1,))
    for mask in by_size[:-1]:
        accumulate(parent, parent_total.at[ch % 2], 2, ch, mask)
    solve_parent(ch)
    for key in sent:
        hop(*key).wait_send()
    for ch in range(chunks):
        for p in range(2):
            for s in range(pairs - 1):
                pass_drain(ch, p, s)
            half_copy(ch, p).wait_send()
            child_store(ch, p).wait()
        last_copy(ch).wait_send()
        parent_store(ch).wait()


def hand_out(first_in, second_in, first_out, second_out, held, in_sem, out_sem):
    steps = []
    for i, (source, target) in enumerate([(first_in, first_out), (second_in, second_out)]):
        for p in range(2):
            j = 2 * i + p
            place = held.at[j]
            steps.append(
                (
                    pltpu.make_async_copy(source.at[0, p], place, in_sem.at[j]),
                    pltpu.make_async_copy(place, target.at[0, p], out_sem.at[j]),
                )
            )
    for take, _ in steps:
        take.start()
    for take, give in steps:
        take.wait()
        give.start()
    for _, give in steps:
        give.wait()


def per_device(
    slots,
    groups,
    child_inverse,
    border_block,
    child_rhs,
    parent_inverse,
    parent_rhs,
    parent_of,
    owner,
    row_map,
):
    sources = child_rhs.shape[3]
    chunks = sources // LANES
    pairs = groups // 2
    child_rows = child_inverse.shape[2]
    border_rows = border_block.shape[2]
    half_rows = parent_rhs.shape[2]
    out_rows = parent_inverse.shape[2] // 2
    bf16 = jnp.bfloat16
    dma = pltpu.SemaphoreType.DMA
    anywhere = pl.BlockSpec(memory_space=pl.ANY)
    scalars = pl.BlockSpec(memory_space=pltpu.SMEM)
    results = pl.pallas_call(
        functools.partial(kernel, slots, groups),
        out_shape=(
            jax.ShapeDtypeStruct((1, 2, child_rows, sources), bf16),
            jax.ShapeDtypeStruct((1, 2, out_rows, sources), bf16),
        ),
        in_specs=[anywhere] * 5 + [scalars, scalars, anywhere],
        out_specs=(anywhere, anywhere),
        scratch_shapes=[
            pltpu.VMEM(child_inverse.shape[1:], bf16),
            pltpu.VMEM(border_block.shape[1:], bf16),
            pltpu.VMEM(parent_inverse.shape[1:], bf16),
            pltpu.VMEM(parent_rhs.shape[1:], bf16),
            pltpu.VMEM((groups, border_rows), jnp.int32),
            pltpu.VMEM((chunks, 2, slots * child_rows, LANES), bf16),
            pltpu.VMEM((chunks, 2, slots * child_rows, LANES), bf16),
            pltpu.VMEM((chunks, 2, slots * half_rows, LANES), bf16),
            pltpu.VMEM((chunks, 2, pairs * border_rows, LANES), bf16),
            pltpu.VMEM((2 * half_rows, pairs * border_rows), bf16),
            pltpu.VMEM((2, max(child_rows, border_rows), 2 * LANES), jnp.float32),
            pltpu.VMEM((2, 2, 2 * out_rows, 2 * LANES), jnp.float32),
            pltpu.VMEM((2, 2 * half_rows, LANES), jnp.float32),
            pltpu.VMEM((chunks, 2, half_rows, LANES), bf16),
            pltpu.VMEM((chunks, 2, half_rows, LANES), bf16),
            pltpu.VMEM((chunks, 2, out_rows, LANES), bf16),
            pltpu.VMEM((chunks, 2, out_rows, LANES), bf16),
            pltpu.VMEM((2, out_rows, sources), bf16),
            dma((3, chunks, 2, 2, slots)),
            dma((3, chunks, 2, 2, slots)),
            dma((chunks, 2, pairs)),
            dma((chunks, 2, pairs)),
            dma((chunks, 2, pairs)),
            dma((chunks, 2, pairs)),
            dma((chunks, 2)),
            dma((chunks, 2)),
            dma((chunks,)),
            dma((chunks,)),
            dma((5,)),
            dma((2 * chunks,)),
            dma((3 * chunks,)),
        ],
        compiler_params=pltpu.CompilerParams(
            collective_id=0, has_side_effects=True, vmem_limit_bytes=56 * 1024 * 1024
        ),
    )(child_inverse, border_block, child_rhs, parent_inverse, parent_rhs, parent_of.reshape(-1), owner, row_map)
    return pl.pallas_call(
        hand_out,
        out_shape=tuple(jax.ShapeDtypeStruct(one.shape, bf16) for one in results),
        in_specs=[anywhere] * 2,
        out_specs=(anywhere, anywhere),
        scratch_shapes=[pltpu.VMEM((4, child_rows, sources), bf16), dma((4,)), dma((4,))],
        compiler_params=pltpu.CompilerParams(vmem_limit_bytes=56 * 1024 * 1024),
    )(*results)


def solution(mesh):
    in_specs = (
        P("grp", None, "blk", None),
        P("grp", None, "blk", None),
        P("grp", None, "blk", None),
        P("grp", None, "blk", None),
        P("grp", None, "blk", None),
        P(),
        P(),
        P(),
    )
    out_specs = (P("grp", None, "blk", None), P("grp", None, "blk", None))
    return jax.shard_map(
        functools.partial(per_device, mesh.shape["blk"], mesh.shape["grp"]),
        mesh=mesh,
        in_specs=in_specs,
        out_specs=out_specs,
        check_vma=False,
    )
```
